128 devices in a mesh: prow: 8 (over z, y_hi), pcol: 16 (over x, y_lo, core).
Axes of the slice: x: 4, y: 4 (y_hi: 2, y_lo: 2; y = y_hi * 2 + y_lo), z: 4, core: 2. Of those that a mesh axis runs over, the one named last changes fastest.
Arguments:
- pair_act: float32 [512, 512, 128], P('prow', 'pcol'), may hold values from -6 to 6
- token_mask: int32 [512], replicated, may hold values from 0 to 1
- w_proj: bfloat16 [4, 128, 128], replicated, may hold values from -0.5 to 0.5
- w_bias: bfloat16 [128, 4], replicated, may hold values from -30 to 30
- w_out: bfloat16 [128, 128], replicated, may hold values from -0.5 to 0.5
- cotangent: bfloat16 [512, 512, 128], P('prow', 'pcol'), may hold values from -6 to 6
Outputs:
- update: float32 [512, 512, 128], P('prow', 'pcol')
- d_pair: float32 [512, 512, 128], P('prow', 'pcol')
The draws below stay inside these ranges and needn't reach their ends.
All inputs are finite; a program needn't handle non-finite values.
Results may differ from the reference program's by a relative error of at most 0.005.
The reference program's roundings to bfloat16 on the way (of `normed_b`, `attention_low`, `d_att_low` and `d_scores_low`) count: a program that leaves them out, or rounds other values in their place, can miss the bound.
Values may be sent and summed in bfloat16 or wider, within the bound.
No kernel may reach another device: no remote copies, remote signals or barrier semaphores. Data moves between devices by JAX's collectives and lax.ppermute only.
A program may use at most 192 MiB of HBM per device.

```python
import math
import jax
import jax.numpy as jnp
from jax import lax

C = 128
H = 4
HD = 128
N = 512


def draw_token_mask(key, part):
    key = jax.random.fold_in(key, 11)
    values = jax.random.randint(key, (N,), 0, 6)
    live_flag = jnp.where(values > 0, 1, 0)
    first_slot = jnp.arange(N) == 0
    return jnp.where(first_slot, 1, live_flag).astype(jnp.int32)


def draw_w_bias(key, part):
    key = jax.random.fold_in(key, 23)
    noise_key = jax.random.fold_in(key, 0)
    drawn = jax.random.normal(noise_key, (C, H), jnp.float32) * (1.5 / math.sqrt(C))
    return jnp.clip(drawn, -30.0, 30.0).astype(jnp.bfloat16)


def levels(rng, dims, cuts, smallest, largest):
    factor_of = 1.0
    for axis_at, blocks in cuts:
        steps = jax.random.uniform(jax.random.fold_in(jax.random.fold_in(rng, 6), axis_at), (blocks,), jnp.float32, smallest / len(cuts), largest / len(cuts))
        factor_of = factor_of * jnp.repeat(jnp.exp(steps), dims[axis_at] // blocks).reshape((-1,) + (1,) * (len(dims) - 1 - axis_at))
    return factor_of


def normal_values(own_key, shape, scale, most, pieces=(), dtype=jnp.bfloat16):
    values = jax.random.normal(own_key, shape, jnp.float32) * scale
    if len(pieces) > 0:
        values = levels(own_key, shape, pieces, -0.22, 0.18) * values
    return jnp.clip(values, min=-most, max=most).astype(dtype)


def setup_inputs(seed: int = 0) -> dict:
    key_of = jax.random.split(jax.random.key(seed), 7)
    return {
        "pair_act": normal_values(key_of[0], (N, N, C), 1.0, 6.0, ((0, 8), (1, 16)), jnp.float32),
        "token_mask": draw_token_mask(jax.random.fold_in(key_of[6], 71), 0),
        "w_proj": normal_values(key_of[2], (4, C, HD), C ** -0.5, 0.5),
        "w_bias": draw_w_bias(jax.random.fold_in(key_of[6], 71), 0),
        "w_out": normal_values(key_of[4], (HD, C), HD ** -0.5, 0.5),
        "cotangent": normal_values(key_of[5], (N, N, C), 1.0, 6.0, ((0, 8), (1, 16))),
    }


HIGHEST = lax.Precision.HIGHEST
norm_eps = 1e-05
masked_score = -1000000000.0

def normalize(pair_act):
    average = lax.optimization_barrier(jnp.mean(pair_act, axis=-1, keepdims=True))
    centred = pair_act - average
    spread = lax.optimization_barrier(jnp.mean(centred * centred, axis=-1, keepdims=True))
    inverse = lax.rsqrt(spread + norm_eps)
    return (centred * inverse, inverse)

def contract(form, left, right):
    return jnp.einsum(form, left.astype(jnp.float32), right.astype(jnp.float32), precision=HIGHEST)

def reference(pair_act, token_mask, w_proj, w_bias, w_out, cotangent):
    n_tokens = pair_act.shape[0]
    head_dim = w_proj.shape[2] // H
    scale_q = 1.0 / math.sqrt(head_dim)
    normed, inverse = normalize(pair_act)
    normed_b = normed.astype(jnp.bfloat16)
    query_vals = (contract('ijc,cd->ijd', normed_b, w_proj[0]) * scale_q).astype(jnp.bfloat16)
    key_vals = contract('ijc,cd->ijd', normed_b, w_proj[1]).astype(jnp.bfloat16)
    value_vals = contract('ijc,cd->ijd', normed_b, w_proj[2]).astype(jnp.bfloat16)
    gate_act = jax.nn.sigmoid(contract('ijc,cd->ijd', normed_b, w_proj[3]))
    bias_full = contract('jkc,ch->hjk', normed_b, w_bias)
    key_live = token_mask > 0
    block_rows = math.gcd(n_tokens, 16)
    blocks = n_tokens // block_rows

    def split_heads(array):
        return array.reshape(blocks, block_rows, n_tokens, H, head_dim)

    def one_block(bias_grad, inputs):
        query_blk, key_blk, value_blk, gate_blk, cot_blk = inputs
        scores = contract('ijhd,ikhd->ihjk', query_blk, key_blk) + bias_full[None]
        scores = jnp.where(key_live[None, None, None, :], scores, masked_score)
        highest = lax.optimization_barrier(jnp.max(scores, axis=-1, keepdims=True))
        weights = jnp.exp(scores - highest)
        attention = weights / lax.optimization_barrier(jnp.sum(weights, axis=-1, keepdims=True))
        attention_low = attention.astype(jnp.bfloat16)
        attended = contract('ihjk,ikhd->ijhd', attention_low, value_blk).reshape(block_rows, n_tokens, -1)
        mixed = (gate_blk * attended).astype(jnp.bfloat16)
        update_blk = contract('ijd,dc->ijc', mixed, w_out)
        d_mixed = contract('ijc,dc->ijd', cot_blk, w_out)
        d_gate = d_mixed * attended * gate_blk * (1.0 - gate_blk)
        d_attended = d_mixed * gate_blk
        d_att_low = d_attended.astype(jnp.bfloat16).reshape(block_rows, n_tokens, H, head_dim)
        row_delta = lax.optimization_barrier(jnp.sum((d_attended * attended).reshape(block_rows, n_tokens, H, head_dim), axis=-1))
        d_probs = contract('ijhd,ikhd->ihjk', d_att_low, value_blk)
        d_scores = attention * (d_probs - jnp.transpose(row_delta, (0, 2, 1))[..., None])
        d_scores_low = d_scores.astype(jnp.bfloat16)
        d_query = contract('ihjk,ikhd->ijhd', d_scores_low, key_blk)
        d_key = contract('ihjk,ijhd->ikhd', d_scores_low, query_blk)
        d_value = contract('ihjk,ijhd->ikhd', attention_low, d_att_low)
        return (bias_grad + lax.optimization_barrier(jnp.sum(d_scores, axis=0)), (update_blk, d_query, d_key, d_value, d_gate))
    inputs = (split_heads(query_vals), split_heads(key_vals), split_heads(value_vals), gate_act.reshape(blocks, block_rows, n_tokens, -1), cotangent.reshape(blocks, block_rows, n_tokens, -1))
    start_grad = jnp.zeros((H, n_tokens, n_tokens), jnp.float32)
    bias_grad, stacked = lax.scan(one_block, start_grad, inputs)
    update_blocks, d_query, d_key, d_value, d_gate = stacked
    update = update_blocks.reshape(n_tokens, n_tokens, -1)
    d_query = d_query.reshape(n_tokens, n_tokens, -1)
    d_key = d_key.reshape(n_tokens, n_tokens, -1)
    d_value = d_value.reshape(n_tokens, n_tokens, -1)
    d_gate = d_gate.reshape(n_tokens, n_tokens, -1)
    d_normed = contract('ijd,cd->ijc', d_query * scale_q, w_proj[0])
    d_normed = d_normed + contract('ijd,cd->ijc', d_key, w_proj[1])
    d_normed = d_normed + contract('ijd,cd->ijc', d_value, w_proj[2])
    d_normed = d_normed + contract('ijd,cd->ijc', d_gate, w_proj[3])
    d_normed = d_normed + contract('hjk,ch->jkc', bias_grad, w_bias)
    first_mean = lax.optimization_barrier(jnp.mean(d_normed, axis=-1, keepdims=True))
    second_mean = lax.optimization_barrier(jnp.mean(d_normed * normed, axis=-1, keepdims=True))
    d_pair = inverse * (d_normed - first_mean - normed * second_mean)
    return (update, d_pair)
```

```python
import functools
import math

import jax
import jax.numpy as jnp
from jax import lax
from jax.experimental import pallas as pl
from jax.experimental.pallas import tpu as pltpu
from jax.sharding import Mesh, PartitionSpec as P

norm_eps = 1e-05
masked_score = -1000000000.0
F32 = jnp.float32
BF16 = jnp.bfloat16
CHIP = ("x", "yl")
CELL = ("x", "yl", "c")
VMEM_LIMIT = 48 * 1024 * 1024


def dot(left, right):
    return lax.dot_general(left, right, (((1,), (0,)), ((), ())), preferred_element_type=F32)


def dot_t(left, right):
    return lax.dot_general(left, right, (((1,), (1,)), ((), ())), preferred_element_type=F32)


def lanes(shape):
    return lax.broadcasted_iota(jnp.int32, shape, len(shape) - 1)


def project_kernel(half, scale_q, where_ref, own_ref, other_ref, live_ref, w_in_ref, w_dm_ref, qd_ref, kv_ref, kvm_ref, ge_ref):
    chips, _, cells, wide = own_ref.shape
    width = wide // 2
    first = where_ref[0] == 0
    own, other = own_ref[:, 0], other_ref[:, 0]
    tokens = jnp.stack([jnp.where(first, own, other), jnp.where(first, other, own)], axis=1)
    tokens = tokens.reshape(chips * 2 * cells, wide)
    normed_b, cot = tokens[:, :width], tokens[:, width:]
    both = dot(normed_b, w_in_ref[...])
    q_gate, key_value = both[:, : 2 * half], both[:, 2 * half :]
    low = lanes(q_gate.shape) < half
    gate = jax.nn.sigmoid(q_gate)
    d_att = dot(cot, w_dm_ref[...]) * gate
    qd_ref[0] = jnp.where(low, q_gate * scale_q, d_att).astype(BF16)
    key_value = key_value.astype(BF16)
    kv_ref[0] = key_value
    kvm_ref[0] = jnp.where(low & (live_ref[...] == 0), 0.0, key_value.astype(F32)).astype(BF16)
    ge_ref[0] = jnp.where(low, pltpu.roll(gate, half, 1), d_att)


def attend_kernel(half, head_dim, first_call, where_ref, qd_ref, kv_ref, kvm_ref, ge_ref, bias_ref, *refs):
    n_in = 0 if first_call else 3
    dkv_in_ref = None if first_call else refs[0]
    mix_ref, dqg_ref, dkv_ref, dbias_ref = refs[n_in:]
    heads = half // head_dim
    row = pl.program_id(0)
    rows_j = qd_ref.shape[1]
    lane = lanes((rows_j, 2 * half))
    qd = qd_ref[0]
    qd_t = qd.astype(F32).T.astype(BF16)
    ge = ge_ref[0]
    gate = pltpu.roll(ge, half, 1)
    kv = kv_ref[0]
    kvm = kvm_ref[0]
    attended = jnp.zeros((rows_j, 2 * half), F32)
    probs = []
    for h in range(heads):
        mine = (lane >= h * head_dim) & (lane < (h + 1) * head_dim)
        scores = dot_t(jnp.where(mine, qd, jnp.zeros_like(qd)), kvm) + bias_ref[h]
        weights = jnp.exp(scores - jnp.max(scores, axis=-1, keepdims=True))
        attention = weights * (1.0 / jnp.sum(weights, axis=-1, keepdims=True))
        attention_low = attention.astype(BF16)
        probs.append((attention, attention_low))
        up = (lane >= half + h * head_dim) & (lane < half + (h + 1) * head_dim)
        attended = jnp.where(up, dot(attention_low, kv), attended)
    edge = ge * attended
    d_gate = edge * (1.0 - gate)
    mixed = gate * attended
    mixed = jnp.where(lane >= half, mixed, 0.0)
    mixed = jnp.where(where_ref[0] == 0, pltpu.roll(mixed, half, 1), mixed)
    mix_ref[0] = mixed.astype(BF16)
    d_query = jnp.zeros((rows_j, 2 * half), F32)
    grads_k, grads_v = [], []
    for h in range(heads):
        attention, attention_low = probs[h]
        mine = (lane >= h * head_dim) & (lane < (h + 1) * head_dim)
        up = (lane >= half + h * head_dim) & (lane < half + (h + 1) * head_dim)
        delta = jnp.sum(jnp.where(up, edge, 0.0), axis=-1, keepdims=True)
        d_probs = dot_t(jnp.where(up, qd, jnp.zeros_like(qd)), kvm)
        d_scores = attention * (d_probs - delta)

        @pl.when(row == 0)
        def _():
            dbias_ref[h] = d_scores

        @pl.when(row > 0)
        def _():
            dbias_ref[h] = dbias_ref[h] + d_scores

        d_low = d_scores.astype(BF16)
        d_query = jnp.where(mine, dot(d_low, kv), d_query)
        grads_k.append(dot(qd_t[h * head_dim : (h + 1) * head_dim], d_low))
        grads_v.append(dot(qd_t[half + h * head_dim : half + (h + 1) * head_dim], attention_low))
    dqg_ref[0] = jnp.where(lane < half, d_query, d_gate)
    grads = jnp.concatenate(grads_k + grads_v, axis=0)
    dkv_ref[0] = grads if first_call else dkv_in_ref[0] + grads


def combine_kernel(half, scale_q, dqg_ref, dkv_ref, w_back_ref, out_ref):
    dqg = dqg_ref[0]
    dqg = jnp.where(lanes(dqg.shape) < half, dqg * scale_q, dqg)
    grads = jnp.concatenate([dqg, dkv_ref[0].T], axis=1)
    high = grads.astype(BF16)
    low = (grads - high.astype(F32)).astype(BF16)
    w_back = w_back_ref[...]
    total = dot(high, w_back) + dot(low, w_back)
    chips, _, _, cells, width = out_ref.shape
    out_ref[:, :, 0] = total.reshape(chips, 2, cells, width)


def normalize(pair_act):
    average = jnp.mean(pair_act, axis=-1, keepdims=True)
    centred = pair_act - average
    spread = jnp.mean(centred * centred, axis=-1, keepdims=True)
    inverse = lax.rsqrt(spread + norm_eps)
    return (centred * inverse, inverse)


def shifted(array, axis, step):
    size = lax.axis_size(axis)
    return lax.ppermute(array, axis, [(s, (s + step) % size) for s in range(size)])


def params(**more):
    return pltpu.CompilerParams(vmem_limit_bytes=VMEM_LIMIT, **more)


def body(pair_act, token_mask, w_proj, w_bias, w_out, cotangent):
    rows, cells, width = pair_act.shape
    n_heads = w_bias.shape[1]
    head_dim = w_proj.shape[2] // n_heads
    my_heads = n_heads // 2
    half = my_heads * head_dim
    scale_q = 1.0 / math.sqrt(head_dim)
    nx, nyl, nz, nyh = (lax.axis_size(a) for a in ("x", "yl", "z", "yh"))
    chips = nx * nyl
    own_rows = rows // chips
    n_tokens = chips * 2 * cells
    core, z_at, yh_at = lax.axis_index("c"), lax.axis_index("z"), lax.axis_index("yh")
    cell_at = lax.axis_index(CELL)
    block_j = nyh * rows

    normed, inverse = normalize(pair_act)
    normed_b = normed.astype(BF16)
    sent = jnp.concatenate([normed_b, cotangent], axis=-1).reshape(chips, own_rows, cells, 2 * width)
    own = lax.all_to_all(sent, CHIP, 0, 0)
    other = shifted(own, "c", 1)

    bias = jnp.einsum("ijc,ch->hij", normed_b, w_bias, preferred_element_type=F32)
    live_here = lax.dynamic_slice_in_dim(token_mask, cell_at * cells, cells) > 0
    bias = jnp.where(live_here[None, None, :], bias, masked_score)
    bias = jnp.broadcast_to(bias.reshape(1, 2, my_heads, rows, cells), (chips, 2, my_heads, rows, cells))
    bias = bias.reshape(chips * 2, my_heads * rows * cells // 128, 128)
    bias = lax.all_to_all(bias, CELL, 0, 0).reshape(chips * 2, my_heads, rows, cells)
    bias = jnp.transpose(bias, (1, 2, 0, 3)).reshape(my_heads, rows, n_tokens)
    bias_far = shifted(bias, "yh", 1)
    low_yh = yh_at == 0
    bias = jnp.concatenate([jnp.where(low_yh, bias, bias_far), jnp.where(low_yh, bias_far, bias)], axis=1)
    bias_of = [bias] + [shifted(bias, "z", nz - s) for s in range(1, nz)]

    def mine(w):
        return lax.dynamic_slice_in_dim(w, core * half, half, 1)

    wq, wk, wv, wg = (mine(w_proj[n]) for n in range(4))
    w_in = jnp.concatenate([wq, wg, wk, wv], axis=1)
    w_back = jnp.concatenate([wq, wg, wk, wv], axis=1).T
    w_out_mine = lax.dynamic_slice_in_dim(w_out, core * half, half, 0)
    w_dm = jnp.concatenate([jnp.zeros((width, half), BF16), w_out_mine.T], axis=1)
    live = jnp.broadcast_to(token_mask[:, None], (n_tokens, 2 * half))

    lane_shape = (own_rows, n_tokens, 2 * half)
    whole = lambda shape: pl.BlockSpec(shape, lambda r, w: (0,) * len(shape))
    per_row = pl.BlockSpec((1, n_tokens, 2 * half), lambda r, w: (r, 0, 0))
    arrived = pl.BlockSpec((chips, 1, cells, 2 * width), lambda r, w: (0, r, 0, 0))
    qd, kv, kvm, ge = pl.pallas_call(
        functools.partial(project_kernel, half, scale_q),
        grid_spec=pltpu.PrefetchScalarGridSpec(
            num_scalar_prefetch=1,
            grid=(own_rows,),
            in_specs=[arrived, arrived, whole(live.shape), whole(w_in.shape), whole(w_dm.shape)],
            out_specs=[per_row] * 4,
        ),
        out_shape=[jax.ShapeDtypeStruct(lane_shape, t) for t in (BF16, BF16, BF16, F32)],
        compiler_params=params(),
        name="project",
    )(core[None], own, other, live, w_in, w_dm)

    mix = dqg = dkv = None
    d_bias = []
    for s in range(nz):
        first_call = s == 0
        where = jnp.stack([core, (z_at + s) % nz])
        at_block = pl.BlockSpec((1, block_j, 2 * half), lambda r, w: (r, w[1], 0))
        dkv_spec = pl.BlockSpec((1, 2 * half, n_tokens), lambda r, w: (r, 0, 0))
        bias_spec = pl.BlockSpec((my_heads, block_j, n_tokens), lambda r, w: (0, 0, 0))
        anywhere = pl.BlockSpec(memory_space=pl.ANY)
        more = () if first_call else (dkv, mix, dqg)
        mix, dqg, dkv, d_block = pl.pallas_call(
            functools.partial(attend_kernel, half, head_dim, first_call),
            grid_spec=pltpu.PrefetchScalarGridSpec(
                num_scalar_prefetch=1,
                grid=(own_rows,),
                in_specs=[at_block, per_row, per_row, at_block, bias_spec]
                + ([] if first_call else [dkv_spec, anywhere, anywhere]),
                out_specs=[at_block, at_block, dkv_spec, bias_spec],
            ),
            out_shape=[
                jax.ShapeDtypeStruct(lane_shape, BF16),
                jax.ShapeDtypeStruct(lane_shape, F32),
                jax.ShapeDtypeStruct((own_rows, 2 * half, n_tokens), F32),
                jax.ShapeDtypeStruct((my_heads, block_j, n_tokens), F32),
            ],
            input_output_aliases={} if first_call else {6: 2, 7: 0, 8: 1},
            compiler_params=params(),
            name=f"attend{s}",
        )(where, qd, kv, kvm, ge, bias_of[s], *more)
        d_bias.append(d_block)

    d_bias = [d_bias[0]] + [shifted(d_bias[s], "z", s) for s in range(1, nz)]
    d_bias = sum(d_bias[1:], d_bias[0]).reshape(my_heads, nyh, rows, n_tokens)
    keep = lax.dynamic_index_in_dim(d_bias, yh_at, 1, keepdims=False)
    give = lax.dynamic_index_in_dim(d_bias, 1 - yh_at, 1, keepdims=False)
    d_bias = keep + shifted(give, "yh", 1)
    d_bias = jnp.transpose(d_bias.reshape(my_heads, rows, chips * 2, cells), (2, 0, 1, 3))
    d_bias = lax.all_to_all(d_bias.reshape(chips * 2, my_heads * rows * cells // 128, 128), CELL, 0, 0)
    d_bias = d_bias.reshape(chips, 2, my_heads * rows * cells // 128, 128).sum(axis=0)
    d_bias = d_bias.reshape(n_heads, rows, cells)

    partial_shape = (chips, 2, own_rows, cells, width)
    partial = pl.pallas_call(
        functools.partial(combine_kernel, half, scale_q),
        grid_spec=pltpu.PrefetchScalarGridSpec(
            num_scalar_prefetch=0,
            grid=(own_rows,),
            in_specs=[
                pl.BlockSpec((1, n_tokens, 2 * half), lambda r: (r, 0, 0)),
                pl.BlockSpec((1, 2 * half, n_tokens), lambda r: (r, 0, 0)),
                pl.BlockSpec(w_back.shape, lambda r: (0, 0)),
            ],
            out_specs=pl.BlockSpec((chips, 2, 1, cells, width), lambda r: (0, 0, r, 0, 0)),
        ),
        out_shape=jax.ShapeDtypeStruct(partial_shape, F32),
        compiler_params=params(),
        name="combine",
    )(dqg, dkv, w_back)

    def to_cells(array):
        keep = lax.dynamic_index_in_dim(array, core, 1, keepdims=False)
        give = lax.dynamic_index_in_dim(array, 1 - core, 1, keepdims=False)
        return lax.all_to_all(keep + shifted(give, "c", 1), CHIP, 0, 0).reshape(rows, cells, width)

    mix = jnp.transpose(mix.reshape(own_rows, chips, 2, cells, width), (1, 2, 0, 3, 4))
    mixed = to_cells(mix)
    update = jnp.einsum("ijd,dc->ijc", mixed, w_out, preferred_element_type=F32)
    d_normed = to_cells(partial)
    d_normed = d_normed + jnp.einsum(
        "hij,ch->ijc", d_bias, w_bias.astype(F32), precision=lax.Precision.HIGHEST
    )
    first_mean = jnp.mean(d_normed, axis=-1, keepdims=True)
    second_mean = jnp.mean(d_normed * normed, axis=-1, keepdims=True)
    d_pair = inverse * (d_normed - first_mean - normed * second_mean)
    return (update, d_pair)


def solution(mesh):
    fine = Mesh(mesh.devices.reshape(4, 2, 4, 2, 2), ("z", "yh", "x", "yl", "c"))
    cells = P(("z", "yh"), CELL, None)
    return jax.shard_map(
        body,
        mesh=fine,
        in_specs=(cells, P(), P(), P(), P(), cells),
        out_specs=(cells, cells),
        check_vma=False,
    )
```

```python
import functools
import math

import jax
import jax.numpy as jnp
from jax import lax
from jax.experimental import pallas as pl
from jax.experimental.pallas import tpu as pltpu
from jax.sharding import Mesh, PartitionSpec as P

norm_eps = 1e-05
masked_score = -1000000000.0
F32 = jnp.float32
BF16 = jnp.bfloat16
CHIP = ("x", "yl")
CELL = ("x", "yl", "c")
NEAR = ("yh", "x", "yl", "c")


def dot(left, right):
    return lax.dot_general(left, right, (((1,), (0,)), ((), ())), preferred_element_type=F32)


def dot_t(left, right):
    return lax.dot_general(left, right, (((1,), (1,)), ((), ())), preferred_element_type=F32)


def dot_exact(left, right):
    high = left.astype(BF16)
    low = (left - high.astype(F32)).astype(BF16)
    return dot(high, right) + dot(low, right)


def lanes(shape):
    return lax.broadcasted_iota(jnp.int32, shape, len(shape) - 1)


def normalize(pair_act):
    average = jnp.mean(pair_act, axis=-1, keepdims=True)
    centred = pair_act - average
    spread = jnp.mean(centred * centred, axis=-1, keepdims=True)
    inverse = lax.rsqrt(spread + norm_eps)
    return (centred * inverse, inverse)


def prepare_kernel(pair_ref, cot_ref, live_ref, w_spread_ref, sent_ref, bias_ref):
    rows, cells, width = pair_ref.shape
    lanes_of_head = w_spread_ref.shape[1] // 4
    step = pl.program_id(0)
    normed_b = normalize(pair_ref[...])[0].astype(BF16)
    sent_ref[0, :, :, :width] = normed_b
    sent_ref[0, :, :, width:] = cot_ref[...]
    spread = dot(normed_b.reshape(rows * cells, width), w_spread_ref[...]).reshape(rows, cells, -1)
    lane = lanes(spread.shape[1:])
    for c in range(2):
        half = slice(c * width, (c + 1) * width)
        total = bias_ref[c]
        for r in range(rows):
            here = lax.rem(lane[:, half], lanes_of_head) == step * rows + r
            total = jnp.where(here, jnp.where(live_ref[...] > 0, spread[r, :, half], masked_score), total)
        bias_ref[c] = total

    @pl.when(step == pl.num_programs(0) - 1)
    def _():
        for n in range(2, bias_ref.shape[0]):
            bias_ref[n] = bias_ref[n % 2]


def after_kernel(*refs):
    pass


def turn_kernel(where_ref, came_ref, *out_refs):
    for t in range(2):
        block = came_ref[lax.rem(where_ref[2] + t, 2)].T
        rows = block.shape[0] // len(out_refs)
        for h, out_ref in enumerate(out_refs):
            out_ref[t * rows : (t + 1) * rows] = block[h * rows : (h + 1) * rows]


def turn_back_kernel(where_ref, before_ref, stacked_ref, *refs):
    terms, out_ref = refs[:-1], refs[-1]
    totals = [stacked_ref[...].sum(axis=0), sum((t[...] for t in terms[1:]), terms[0][...])]
    rows = totals[0].shape[0] // 2
    for t in range(2):
        both = jnp.concatenate([total[t * rows : (t + 1) * rows] for total in totals], axis=0)
        out_ref[lax.rem(where_ref[2] + t, 2)] = both.T.reshape(out_ref.shape[1:])


def weights_kernel(half, where_ref, w_proj_ref, w_out_ref, w_in_ref, w_back_ref, w_dm_ref):
    first = where_ref[0] == 0

    def mine(w):
        w = w.astype(F32)
        return jnp.where(first, w[:, :half], w[:, half:])

    w_in = jnp.concatenate([mine(w_proj_ref[n]) for n in (0, 3, 1, 2)], axis=1)
    w_in_ref[...] = w_in.astype(BF16)
    w_back_ref[...] = w_in.T.astype(BF16)
    w_dm = mine(w_out_ref[...].astype(F32).T)
    w_dm_ref[...] = jnp.concatenate([jnp.zeros_like(w_dm), w_dm], axis=1).astype(BF16)


def project_kernel(half, scale_q, where_ref, own_ref, other_ref, live_ref, w_in_ref, w_dm_ref, qd_ref, kv_ref, kvm_ref, ge_ref):
    chips, _, cells, wide = own_ref.shape
    width = wide // 2
    first = where_ref[0] == 0
    own, other = own_ref[:, 0], other_ref[:, 0]
    tokens = jnp.stack([jnp.where(first, own, other), jnp.where(first, other, own)], axis=1)
    tokens = tokens.reshape(chips * 2 * cells, wide)
    normed_b, cot = tokens[:, :width], tokens[:, width:]
    both = dot(normed_b, w_in_ref[...])
    q_gate, key_value = both[:, : 2 * half], both[:, 2 * half :]
    low = lanes(q_gate.shape) < half
    gate = jax.nn.sigmoid(q_gate)
    d_att = dot(cot, w_dm_ref[...]) * gate
    qd_ref[0] = jnp.where(low, q_gate * scale_q, d_att).astype(BF16)
    key_value = key_value.astype(BF16)
    kv_ref[0] = key_value
    kvm_ref[0] = jnp.where(low & (live_ref[...] == 0), 0.0, key_value.astype(F32)).astype(BF16)
    ge_ref[0] = jnp.where(low, pltpu.roll(gate, half, 1), d_att)


def attend_kernel(half, head_dim, head, scale_q, steps, n_z, z_order, last, where_ref, qd_ref, kv_ref, kvm_ref, ge_ref, *refs):
    bias_refs, refs = refs[: len(steps)], refs[len(steps) :]
    if last:
        (x0_ref, dkv0_ref, w_back_ref), refs = refs[:3], refs[3:]
        (keep_dn_ref, give_dn_ref, keep_mix_ref, give_mix_ref), refs = refs[:4], refs[4:]
    else:
        (x_ref, dkv_ref), refs = refs[1:3], refs[3:]
    *dbias_refs, bias_s, dbias_s = refs
    step = pl.program_id(0)
    rows_j = bias_refs[0].shape[0] // 2
    places = [
        pl.ds(pl.multiple_of((lax.rem(where_ref[1] + s, n_z) * 2 + lax.rem(where_ref[2] + t, 2)) * rows_j, rows_j), rows_j)
        for s in steps
        for t in range(2)
    ]

    @pl.when(step == 0)
    def _():
        for n, p in enumerate(places):
            bias_s[p] = bias_refs[n // 2][(n % 2) * rows_j : (n % 2 + 1) * rows_j]
        dbias_s[...] = jnp.zeros_like(dbias_s)

    first = where_ref[0] == 0
    lane = lanes(qd_ref.shape[1:])
    mine = (lane >= head * head_dim) & (lane < (head + 1) * head_dim)
    up = (lane >= half + head * head_dim) & (lane < half + (head + 1) * head_dim)
    rows = range(qd_ref.shape[0])
    qd = [qd_ref[r] for r in rows]
    kv = [kv_ref[r] for r in rows]
    zero = jnp.zeros_like(qd[0])
    scores = [dot_t(jnp.where(mine, qd[r], zero), kvm_ref[r]) for r in rows]
    d_probs = [dot_t(jnp.where(up, qd[r], zero), kvm_ref[r]) for r in rows]
    qd_t = [qd[r].astype(F32).T.astype(BF16) for r in rows]
    attention, attention_low = [], []
    for r in rows:
        biased = scores[r] + bias_s[...]
        weights = jnp.exp(biased - jnp.max(biased, axis=-1, keepdims=True))
        attention.append(weights * (1.0 / jnp.sum(weights, axis=-1, keepdims=True)))
        attention_low.append(attention[r].astype(BF16))
    attended = [jnp.where(up, dot(attention_low[r], kv[r]), 0.0) for r in rows]
    edge = [ge_ref[r] * attended[r] for r in rows]
    d_scores = [attention[r] * (d_probs[r] - jnp.sum(edge[r], axis=-1, keepdims=True)) for r in rows]
    dbias_s[...] += sum(d_scores[1:], d_scores[0])
    d_low = [d_scores[r].astype(BF16) for r in rows]
    d_query = [dot(d_low[r], kv[r]) * scale_q for r in rows]
    d_key = [dot(qd_t[r][head * head_dim : (head + 1) * head_dim], d_low[r]) for r in rows]
    d_value = [dot(qd_t[r][half + head * head_dim : half + (head + 1) * head_dim], attention_low[r]) for r in rows]
    for r in rows:
        gate = pltpu.roll(ge_ref[r], half, 1)
        mixed = gate * attended[r]
        x = jnp.where(mine, d_query[r], jnp.where(up, edge[r] * (1.0 - gate), pltpu.roll(mixed, 2 * half - head_dim, 1)))
        if not last:
            x_ref[r] = x
            dkv_ref[r] = jnp.concatenate([d_key[r], d_value[r]], axis=0)
            continue
        x0 = x0_ref[r]
        even = (lane < head_dim) | ((lane >= half) & (lane < half + head_dim))
        dqg = jnp.where(even, x0, x)
        mixed = pltpu.roll(jnp.where(lane < half, x0, x), head_dim, 1)
        mixed = jnp.where(lane >= half, mixed, 0.0)
        mixed = jnp.where(first, pltpu.roll(mixed, half, 1), mixed)
        dkv0 = dkv0_ref[r]
        grads = [dkv0[:head_dim], d_key[r], dkv0[head_dim:], d_value[r]]
        grads = jnp.concatenate([dqg, jnp.concatenate(grads, axis=0).T], axis=1)
        d_normed = dot_exact(grads, w_back_ref[...])
        chips, _, cells, width = keep_dn_ref.shape
        d_normed = d_normed.reshape(chips, 2, cells, width)
        mixed = mixed.reshape(chips, 2, cells, width)
        keep_dn_ref[:, r] = jnp.where(first, d_normed[:, 0], d_normed[:, 1])
        give_dn_ref[:, r] = jnp.where(first, d_normed[:, 1], d_normed[:, 0])
        keep_mix_ref[:, r] = jnp.where(first, mixed[:, 0], mixed[:, 1]).astype(BF16)
        give_mix_ref[:, r] = jnp.where(first, mixed[:, 1], mixed[:, 0]).astype(BF16)

    @pl.when(step == pl.num_programs(0) - 1)
    def _():
        for n, p in enumerate(places):
            part = slice((n % 2) * rows_j, (n % 2 + 1) * rows_j)
            if z_order:
                dbias_refs[0][lax.rem(where_ref[1] + steps[n // 2], n_z), part] = dbias_s[p]
            else:
                dbias_refs[n // 2][part] = dbias_s[p]


def merge_kernel(keep_dn_ref, came_dn_ref, keep_mix_ref, came_mix_ref, out_ref):
    width = keep_dn_ref.shape[-1]
    d_normed = keep_dn_ref[...] + came_dn_ref[...]
    high = d_normed.astype(BF16)
    out_ref[..., :width] = keep_mix_ref[...] + came_mix_ref[...]
    out_ref[..., width : 2 * width] = high
    out_ref[..., 2 * width :] = (d_normed - high.astype(F32)).astype(BF16)


def finish_kernel(pair_ref, came_ref, dbias_ref, w_out_ref, w_spread_ref, update_ref, dpair_ref, dbias_s):
    rows, cells, width = pair_ref.shape
    flat = (rows * cells, width)
    lanes_of_head = w_spread_ref.shape[0] // 4
    step = pl.program_id(0)

    @pl.when(step == 0)
    def _():
        for c in range(2):
            total = dbias_ref[c]
            for n in range(c + 2, dbias_ref.shape[0], 2):
                total = total + dbias_ref[n]
            dbias_s[:, c * width : (c + 1) * width] = total

    normed, inverse = normalize(pair_ref[...].reshape(flat))
    came = came_ref[0].reshape(rows * cells, 3 * width)
    update_ref[...] = dot(came[:, :width], w_out_ref[...]).reshape(pair_ref.shape)
    d_bias = dbias_s[...]
    own = lax.rem(lanes(d_bias.shape), lanes_of_head)
    picked = [jnp.where(own == step * rows + r, d_bias, 0.0) for r in range(rows)]
    picked = jnp.concatenate(picked, axis=0)
    from_bias = jnp.zeros(flat, F32)
    for _ in range(3):
        high = picked.astype(BF16)
        from_bias = from_bias + dot(high, w_spread_ref[...])
        picked = picked - high.astype(F32)
    d_normed = came[:, width : 2 * width].astype(F32) + came[:, 2 * width :].astype(F32) + from_bias
    first_mean = jnp.mean(d_normed, axis=-1, keepdims=True)
    second_mean = jnp.mean(d_normed * normed, axis=-1, keepdims=True)
    dpair_ref[...] = (inverse * (d_normed - first_mean - normed * second_mean)).reshape(pair_ref.shape)


def shifted(array, axis, step):
    size = lax.axis_size(axis)
    return lax.ppermute(array, axis, [(s, (s + step) % size) for s in range(size)])


def kernel(fn, grid, in_specs, out_specs, out_shape, micros, name, scalars=0, scratch=(), aliases=None, vmem=24):
    return pl.pallas_call(
        fn,
        grid_spec=pltpu.PrefetchScalarGridSpec(
            num_scalar_prefetch=scalars, grid=grid, in_specs=in_specs, out_specs=out_specs, scratch_shapes=scratch
        ),
        out_shape=out_shape,
        input_output_aliases=aliases or {},
        compiler_params=pltpu.CompilerParams(vmem_limit_bytes=vmem * 1024 * 1024),
        cost_estimate=pl.CostEstimate(flops=int(micros * 1.1e9), bytes_accessed=int(micros * 2e6), transcendentals=0),
        name=name,
    )


def body(pair_act, token_mask, w_proj, w_bias, w_out, cotangent):
    rows, cells, width = pair_act.shape
    n_heads = w_bias.shape[1]
    head_dim = w_proj.shape[2] // n_heads
    my_heads = n_heads // 2
    half = my_heads * head_dim
    scale_q = 1.0 / math.sqrt(head_dim)
    nx, nyl, nz = (lax.axis_size(a) for a in ("x", "yl", "z"))
    chips = nx * nyl
    own_rows = rows // chips
    n_tokens = chips * 2 * cells
    core, z_at, yh_at = lax.axis_index("c"), lax.axis_index("z"), lax.axis_index("yh")
    cell_at = lax.axis_index(CELL)
    where = jnp.stack([core, z_at, yh_at])
    shape = jax.ShapeDtypeStruct

    def fixed(dims):
        return pl.BlockSpec(dims, lambda r, *w: (0,) * len(dims))

    by_rows = pl.BlockSpec((own_rows, cells, width), lambda r: (r, 0, 0))
    anywhere = pl.BlockSpec(memory_space=pl.ANY)

    live_here = lax.dynamic_slice_in_dim(token_mask, cell_at * cells, cells)
    live_here = jnp.broadcast_to(live_here[:, None], (cells, width))
    w_spread = jnp.repeat(w_bias, rows, axis=1)
    n_cells = chips * 2
    vmem = pl.BlockSpec(memory_space=pltpu.VMEM)
    cells_of = (2 * n_cells, cells, my_heads * rows)
    sent, bias = kernel(
        prepare_kernel, (chips,),
        [by_rows, by_rows, fixed(live_here.shape), fixed(w_spread.shape)],
        [pl.BlockSpec((1, own_rows, cells, 2 * width), lambda r: (r, 0, 0, 0)), fixed(cells_of)],
        [shape((chips, own_rows, cells, 2 * width), BF16), shape(cells_of, F32)],
        3, "prepare",
    )(pair_act, cotangent, live_here, w_spread)

    bias = lax.all_to_all(bias, NEAR, 0, 0)
    sent = kernel(
        after_kernel, (), [anywhere, anywhere], anywhere, shape(sent.shape, sent.dtype), 0.1, "after", aliases={0: 0}
    )(sent, bias)
    block_shape = (2 * rows, n_tokens)
    blocks = kernel(
        turn_kernel, (1,), [fixed((2, n_tokens, my_heads * rows))], [fixed(block_shape)] * my_heads,
        [shape(block_shape, F32)] * my_heads, 1, "turn", scalars=1,
    )(where, bias.reshape(2, n_tokens, my_heads * rows))
    up = [shifted(block, "z", nz - 1) for block in blocks]
    down = [shifted(block, "z", 1) for block in blocks]
    across = [shifted(up[0], "z", nz - 1), shifted(down[1], "z", 1)]
    bias_of = [[blocks[h], up[h], across[h], down[h]] for h in range(my_heads)]

    w_in, w_back, w_dm = kernel(
        functools.partial(weights_kernel, half), (1,), [fixed(w_proj.shape), fixed(w_out.shape)],
        [fixed((width, 4 * half)), fixed((4 * half, width)), fixed((width, 2 * half))],
        [shape((width, 4 * half), BF16), shape((4 * half, width), BF16), shape((width, 2 * half), BF16)],
        1, "weights", scalars=1,
    )(where, w_proj, w_out)
    live = jnp.broadcast_to(token_mask[:, None], (n_tokens, 2 * half))

    own = lax.all_to_all(sent, CHIP, 0, 0)
    own = kernel(
        after_kernel, (), [anywhere] * 7, anywhere, shape(own.shape, own.dtype), 0.1, "after_own", aliases={0: 0}
    )(own, *up, *down, w_in, live)
    other = shifted(own, "c", 1)

    lane_shape = (own_rows, n_tokens, 2 * half)
    per_row = pl.BlockSpec((1, n_tokens, 2 * half), lambda r, w: (r, 0, 0))
    arrived = pl.BlockSpec((chips, 1, cells, 2 * width), lambda r, w: (0, r, 0, 0))
    qd, kv, kvm, ge = kernel(
        functools.partial(project_kernel, half, scale_q), (own_rows,),
        [arrived, arrived, fixed(live.shape), fixed(w_in.shape), fixed(w_dm.shape)],
        [per_row] * 4,
        [shape(lane_shape, t) for t in (BF16, BF16, BF16, F32)],
        0.1, "project", scalars=1,
    )(where, own, other, live, w_in, w_dm)

    per_row = pl.BlockSpec((2, n_tokens, 2 * half), lambda r, w: (r, 0, 0))
    dkv_spec = pl.BlockSpec((2, 2 * head_dim, n_tokens), lambda r, w: (r, 0, 0))
    cell_spec = pl.BlockSpec((chips, 2, cells, width), lambda r, w: (0, r, 0, 0))
    cell_shape = (chips, own_rows, cells, width)
    blocks = [fixed(block_shape)] * nz
    stacked = (nz,) + block_shape
    block_outs = [shape(block_shape, F32)] * nz
    attend = functools.partial(attend_kernel, half, head_dim)
    x_shapes = [shape(lane_shape, F32), shape((own_rows, 2 * head_dim, n_tokens), F32)]
    x0, dkv0, d_bias0 = kernel(
        functools.partial(attend, 0, scale_q, range(nz), nz, True, False), (own_rows // 2,),
        [per_row] * 4 + blocks + [anywhere],
        [per_row, dkv_spec, fixed(stacked)],
        x_shapes + [shape(stacked, F32)],
        11, "attend0", scalars=1, vmem=60,
        scratch=[pltpu.VMEM((n_tokens, n_tokens), F32)] * 2,
    )(where, qd, kv, kvm, ge, *bias_of[0], across[1])
    d_bias0 = lax.all_to_all(d_bias0, "z", 0, 0)
    keep_dn, give_dn, keep_mix, give_mix, *d_bias1 = kernel(
        functools.partial(attend, 1, scale_q, range(nz), nz, False, True), (own_rows // 2,),
        [per_row] * 4 + blocks + [per_row, dkv_spec, fixed(w_back.shape)],
        [cell_spec] * 4 + blocks,
        [shape(cell_shape, t) for t in (F32, F32, BF16, BF16)] + block_outs,
        0.1, "attend1", scalars=1, vmem=60,
        scratch=[pltpu.VMEM((n_tokens, n_tokens), F32)] * 2,
    )(where, qd, kv, kvm, ge, *bias_of[1], x0, dkv0, w_back)

    give_dn, give_mix = kernel(
        after_kernel, (), [anywhere] * 3, [anywhere] * 2,
        [shape(cell_shape, F32), shape(cell_shape, BF16)], 0.1, "after_give", aliases={0: 0, 1: 1},
    )(give_dn, give_mix, d_bias0)
    came_dn, came_mix = shifted(give_dn, "c", 1), shifted(give_mix, "c", 1)
    cell_block = pl.BlockSpec((1, own_rows, cells, width), lambda r: (r, 0, 0, 0))
    wide_block = pl.BlockSpec((1, own_rows, cells, 3 * width), lambda r: (r, 0, 0, 0))
    merged = kernel(
        merge_kernel, (chips,), [cell_block] * 4, wide_block,
        shape((chips, own_rows, cells, 3 * width), BF16), 2, "merge",
    )(keep_dn, came_dn, keep_mix, came_mix)
    back = lax.all_to_all(merged, CHIP, 0, 0)

    came = [shifted(d_bias1[s], "z", s) for s in range(1, nz)]
    by_yh = (2, n_cells, cells, my_heads * rows)
    d_bias = kernel(
        turn_back_kernel, (1,), [anywhere, fixed(stacked)] + blocks, fixed(by_yh), shape(by_yh, F32),
        1, "turn_back", scalars=1,
    )(where, back, d_bias0, d_bias1[0], *came)
    d_bias = lax.all_to_all(d_bias.reshape(cells_of), NEAR, 0, 0)

    return kernel(
        finish_kernel, (chips,),
        [by_rows, wide_block, fixed(cells_of), fixed(w_out.shape), fixed((n_heads * rows, width))],
        [by_rows, by_rows],
        [shape(pair_act.shape, F32)] * 2,
        3, "finish", scratch=[pltpu.VMEM((cells, n_heads * rows), F32)],
    )(pair_act, back, d_bias, w_out, w_spread.T)


def solution(mesh):
    fine = Mesh(mesh.devices.reshape(4, 2, 4, 2, 2), ("z", "yh", "x", "yl", "c"))
    cells = P(("z", "yh"), CELL, None)
    return jax.shard_map(
        body,
        mesh=fine,
        in_specs=(cells, P(), P(), P(), P(), cells),
        out_specs=(cells, cells),
        check_vma=False,
    )
```

```python
import functools
import math

import jax
import jax.numpy as jnp
from jax import lax
from jax.experimental import pallas as pl
from jax.experimental.pallas import tpu as pltpu
from jax.sharding import Mesh, PartitionSpec as P

norm_eps = 1e-05
masked_score = -1000000000.0
code_top = 32000.0
RA = 2
RB = 2
GP = 4
GM = 4
GF = 4
F32 = jnp.float32
BF16 = jnp.bfloat16
CHIP = ("x", "yl")
CELL = ("x", "yl", "c")
NEAR = ("yh", "x", "yl", "c")


def dot(left, right):
    return lax.dot_general(left, right, (((1,), (0,)), ((), ())), preferred_element_type=F32)


def dot_t(left, right):
    return lax.dot_general(left, right, (((1,), (1,)), ((), ())), preferred_element_type=F32)


def dot_exact(left, right):
    high = left.astype(BF16)
    low = (left - high.astype(F32)).astype(BF16)
    return dot(high, right) + dot(low, right)


def lanes(shape):
    return lax.broadcasted_iota(jnp.int32, shape, len(shape) - 1)


def normalize(pair_act):
    average = jnp.mean(pair_act, axis=-1, keepdims=True)
    centred = pair_act - average
    spread = jnp.mean(centred * centred, axis=-1, keepdims=True)
    inverse = lax.rsqrt(spread + norm_eps)
    return (centred * inverse, inverse)


def prepare_kernel(pair_ref, cot_ref, live_ref, w_spread_ref, sent_ref, bias_ref):
    rows, cells, width = pair_ref.shape
    lanes_of_head = w_spread_ref.shape[1] // 4
    step = pl.program_id(0)
    normed_b = normalize(pair_ref[...])[0].astype(BF16)
    sent_ref[..., :width] = normed_b.reshape(sent_ref.shape[:-1] + (width,))
    sent_ref[..., width:] = cot_ref[...].reshape(sent_ref.shape[:-1] + (width,))
    spread = dot(normed_b.reshape(rows * cells, width), w_spread_ref[...]).reshape(rows, cells, -1)
    lane = lanes(spread.shape[1:])
    for c in range(2):
        half = slice(c * width, (c + 1) * width)
        total = bias_ref[c]
        for r in range(rows):
            here = lax.rem(lane[:, half], lanes_of_head) == step * rows + r
            total = jnp.where(here, jnp.where(live_ref[...] > 0, spread[r, :, half], masked_score), total)
        bias_ref[c] = total

    @pl.when(step == pl.num_programs(0) - 1)
    def _():
        for n in range(2, bias_ref.shape[0]):
            bias_ref[n] = bias_ref[n % 2]


def after_kernel(*refs):
    pass


def turn_kernel(where_ref, came_ref, out_ref):
    rows = out_ref.shape[1] // 2
    for t in range(2):
        block = came_ref[lax.rem(where_ref[2] + t, 2)].T
        for h in range(out_ref.shape[0]):
            out_ref[h, t * rows : (t + 1) * rows] = block[h * rows : (h + 1) * rows]


def turn_back_kernel(where_ref, before_ref, *refs):
    late_ref, *terms, out_ref = refs
    total = sum((t[...] for t in terms[1:]), terms[0][...])
    n_tokens = total.shape[-1]
    quarters = late_ref[..., n_tokens:].astype(jnp.int32).astype(F32)
    total = total + decode(late_ref[..., :n_tokens], jnp.max(quarters, axis=-1, keepdims=True))
    rows = total.shape[1] // 2
    for t in range(2):
        both = total[:, t * rows : (t + 1) * rows].reshape(total.shape[0] * rows, -1)
        out_ref[lax.rem(where_ref[2] + t, 2)] = both.T.reshape(out_ref.shape[1:])


def weights_kernel(half, where_ref, w_proj_ref, w_out_ref, w_in_ref, w_back_ref, w_dm_ref):
    first = where_ref[0] == 0

    def mine(w):
        w = w.astype(F32)
        return jnp.where(first, w[:, :half], w[:, half:])

    w_in = jnp.concatenate([mine(w_proj_ref[n]) for n in (0, 3, 1, 2)], axis=1)
    w_in_ref[...] = w_in.astype(BF16)
    w_back_ref[...] = w_in.T.astype(BF16)
    w_dm = mine(w_out_ref[...].astype(F32).T)
    w_dm_ref[...] = jnp.concatenate([jnp.zeros_like(w_dm), w_dm], axis=1).astype(BF16)


def project(half, scale_q, first, own, other, live, w_in, w_dm):
    chips, cells, wide = own.shape
    width = wide // 2
    tokens = jnp.stack([jnp.where(first, own, other), jnp.where(first, other, own)], axis=1)
    tokens = tokens.reshape(chips * 2 * cells, wide)
    normed_b, cot = tokens[:, :width], tokens[:, width:]
    both = dot(normed_b, w_in)
    q_gate, key_value = both[:, : 2 * half], both[:, 2 * half :]
    low = lanes(q_gate.shape) < half
    gate = jax.nn.sigmoid(q_gate)
    d_att = dot(cot, w_dm) * gate
    qd = jnp.where(low, q_gate * scale_q, d_att).astype(BF16)
    kv = key_value.astype(BF16)
    kvm = jnp.where(low & (live == 0), 0.0, kv.astype(F32)).astype(BF16)
    return qd, kv, kvm, jnp.where(low, pltpu.roll(gate, half, 1), d_att)


def encode(values):
    most = jnp.maximum(jnp.max(jnp.abs(values), axis=-1, keepdims=True), 1e-30)
    quarters = jnp.floor(jnp.log(most) * (4.0 / math.log(2.0))) + 2.0
    codes = jnp.floor(values * (code_top * jnp.exp2(quarters * -0.25)) + 0.5)
    return codes.astype(jnp.int32).astype(jnp.int16), quarters


def decode(codes, quarters):
    return codes.astype(jnp.int32).astype(F32) * (jnp.exp2(quarters * 0.25) * (1.0 / code_top))


def attend(half, head_dim, scale_q, rows, bias_refs, dbias_refs):
    heads = range(half // head_dim)
    each = [(r, h) for r in range(len(rows)) for h in heads]
    block = bias_refs[0].shape[1]
    qds, ges, kvs, kvms = zip(*rows)
    lane = lanes(qds[0].shape)
    zero = jnp.zeros_like(qds[0])

    def own(h, base):
        return (lane >= base + h * head_dim) & (lane < base + (h + 1) * head_dim)

    scores = {(r, h): dot_t(jnp.where(own(h, 0), qds[r], zero), kvms[r]) for r, h in each}
    d_probs = {(r, h): dot_t(jnp.where(own(h, half), qds[r], zero), kvms[r]) for r, h in each}
    qd_t = [qd.astype(F32).T.astype(BF16) for qd in qds]
    attention, low = {}, {}
    for r, h in each:
        biased = [scores[r, h][n * block : (n + 1) * block] + ref[h] for n, ref in enumerate(bias_refs)]
        biased = jnp.concatenate(biased, axis=0)
        weights = jnp.exp(biased - jnp.max(biased, axis=-1, keepdims=True))
        attention[r, h] = weights * (1.0 / jnp.sum(weights, axis=-1, keepdims=True))
        low[r, h] = attention[r, h].astype(BF16)
    attended = [jnp.zeros(lane.shape, F32) for _ in rows]
    for r, h in each:
        attended[r] = jnp.where(own(h, half), dot(low[r, h], kvs[r]), attended[r])
    edge = [ge * att for ge, att in zip(ges, attended)]
    d_low = {}
    for h in heads:
        total = None
        for r in range(len(rows)):
            delta = jnp.sum(jnp.where(own(h, half), edge[r], 0.0), axis=-1, keepdims=True)
            d_scores = attention[r, h] * (d_probs[r, h] - delta)
            total = d_scores if total is None else total + d_scores
            d_low[r, h] = d_scores.astype(BF16)
        for n, ref in enumerate(dbias_refs):
            ref[h] += total[n * block : (n + 1) * block]
    results = []
    for r in range(len(rows)):
        gate = pltpu.roll(ges[r], half, 1)
        dqg = edge[r] * (1.0 - gate)
        for h in heads:
            dqg = jnp.where(own(h, 0), dot(d_low[r, h], kvs[r]) * scale_q, dqg)
        d_key = [dot(qd_t[r][h * head_dim : (h + 1) * head_dim], d_low[r, h]) for h in heads]
        d_value = [dot(qd_t[r][half + h * head_dim : half + (h + 1) * head_dim], low[r, h]) for h in heads]
        mixed = jnp.where(lane >= half, gate * attended[r], 0.0)
        results.append((dqg, mixed, jnp.concatenate(d_key + d_value, axis=0)))
    return results


def clear(refs):
    @pl.when(pl.program_id(0) == 0)
    def _():
        for ref in refs:
            ref[...] = jnp.zeros_like(ref)


def places(where_ref, steps, n_z, rows_j):
    at = [lax.rem(where_ref[1] + s, n_z) * 2 + lax.rem(where_ref[2] + t, 2) for s in steps for t in range(2)]
    return [pl.ds(pl.multiple_of(p * rows_j, rows_j), rows_j) for p in at]


def first_kernel(half, head_dim, scale_q, steps, n_z, n_now, where_ref, own_ref, other_ref, live_ref, w_in_ref, w_dm_ref, *refs):
    bias_refs, refs = refs[:n_now], refs[n_now:]
    (qd_ref, kv_ref, kvm_ref, ge_ref, dqg_ref, mix_ref, dkv_ref), refs = refs[:7], refs[7:]
    dbias_refs, (qd_s, ge_s) = refs[:n_now], refs[n_now:]
    clear(dbias_refs)
    weights = (w_in_ref[...], w_dm_ref[...])
    first = where_ref[0] == 0
    rows_j = bias_refs[0].shape[1] // 2
    now = slice(0, dqg_ref.shape[1])
    at = places(where_ref, steps, n_z, rows_j)
    rows = []
    for r in range(qd_ref.shape[0]):
        qd, kv, kvm, ge = project(half, scale_q, first, own_ref[:, r], other_ref[:, r], live_ref[...], *weights)
        kv_ref[r] = kv
        kvm_ref[r] = kvm
        qd_s[r] = qd
        ge_s[r] = ge
        for n, p in enumerate(at):
            here = slice(n * rows_j, (n + 1) * rows_j)
            qd_ref[r, here] = qd_s[r, p]
            ge_ref[r, here] = ge_s[r, p]
        rows.append((qd_ref[r, now], ge_ref[r, now], kv, kvm))
    for r, (dqg, mixed, dkv) in enumerate(attend(half, head_dim, scale_q, rows, bias_refs, dbias_refs)):
        dqg_ref[r] = dqg
        dkv_ref[r] = dkv
        mix_ref[r] = mixed.astype(BF16)


def last_kernel(half, head_dim, scale_q, steps, n_z, where_ref, qd_ref, kv_ref, kvm_ref, ge_ref, bias_ref, dqg_ref, mix_ref, dkv_ref, w_back_ref, *refs):
    (keep_dn_ref, give_dn_ref, keep_mix_ref, give_mix_ref, late_ref, dbias_ref, dn_s, mix_s) = refs
    clear([dbias_ref])
    rows = [(qd_ref[r], ge_ref[r], kv_ref[r], kvm_ref[r]) for r in range(qd_ref.shape[0])]
    results = attend(half, head_dim, scale_q, rows, [bias_ref], [dbias_ref])
    first = where_ref[0] == 0
    w_back = w_back_ref[...]
    rows_j = bias_ref.shape[1] // 2
    at = places(where_ref, steps, n_z, rows_j)
    chips, _, cells, width = keep_dn_ref.shape
    for r, (dqg, mixed, dkv) in enumerate(results):
        dn_s[r] = dot_exact((dkv + dkv_ref[r]).T, w_back[2 * half :])
        from_queries = dot_exact(jnp.concatenate([dqg_ref[r], dqg], axis=0), w_back[: 2 * half])
        mixed = jnp.concatenate([mix_ref[r].astype(F32), mixed], axis=0)
        mixed = jnp.where(first, pltpu.roll(mixed, half, 1), mixed)
        for n, p in enumerate(at):
            here = slice(n * rows_j, (n + 1) * rows_j)
            dn_s[r, p] += from_queries[here]
            mix_s[r, p] = mixed[here]
        d_normed = dn_s[r].reshape(chips, 2, cells, width)
        mixed = mix_s[r].reshape(chips, 2, cells, width)
        keep_dn_ref[:, r] = jnp.where(first, d_normed[:, 0], d_normed[:, 1])
        give_dn_ref[:, r] = jnp.where(first, d_normed[:, 1], d_normed[:, 0])
        keep_mix_ref[:, r] = jnp.where(first, mixed[:, 0], mixed[:, 1]).astype(BF16)
        give_mix_ref[:, r] = jnp.where(first, mixed[:, 1], mixed[:, 0]).astype(BF16)

    @pl.when(pl.program_id(0) == pl.num_programs(0) - 1)
    def _():
        n_tokens = dbias_ref.shape[-1]
        codes, quarters = encode(dbias_ref[...])
        late_ref[..., :n_tokens] = codes
        quarters = jnp.broadcast_to(quarters, codes.shape[:-1] + (late_ref.shape[-1] - n_tokens,))
        late_ref[..., n_tokens:] = quarters.astype(jnp.int32).astype(jnp.int16)


def merge_kernel(before_ref, keep_dn_ref, came_dn_ref, keep_mix_ref, came_mix_ref, out_ref):
    chips, rows, cells, width = keep_dn_ref.shape
    both = (keep_dn_ref[...] + came_dn_ref[...], keep_mix_ref[...].astype(F32) + came_mix_ref[...].astype(F32))
    lane = lanes((cells, width))
    for n, values in enumerate(both):
        at = slice(n * width, (n + 1) * width)
        codes, quarters = encode(values)
        out_ref[:, :rows, :, at] = codes
        for c in range(chips):
            line = jnp.broadcast_to(quarters[c, 0], (cells, width))
            for r in range(1, rows):
                line = jnp.where(lane == r, quarters[c, r], line)
            out_ref[c, rows, :, at] = line.astype(jnp.int32).astype(jnp.int16)


def finish_kernel(pair_ref, came_ref, dbias_ref, w_out_ref, w_spread_ref, update_ref, dpair_ref, dbias_s):
    rows, cells, width = pair_ref.shape
    chips, chip_rows = came_ref.shape[0], came_ref.shape[1] - 1
    flat = (rows * cells, width)
    lanes_of_head = w_spread_ref.shape[0] // 4
    step = pl.program_id(0)

    @pl.when(step == 0)
    def _():
        for c in range(2):
            total = dbias_ref[c].astype(F32)
            for n in range(c + 2, dbias_ref.shape[0], 2):
                total = total + dbias_ref[n].astype(F32)
            dbias_s[:, c * width : (c + 1) * width] = total

    normed, inverse = normalize(pair_ref[...].reshape(flat))
    lane = lanes((cells, width))
    came = []
    for n in range(2):
        at = slice(n * width, (n + 1) * width)
        quarters = []
        for c in range(chips):
            line = came_ref[c, chip_rows, :, at].astype(jnp.int32).astype(F32)
            quarters += [jnp.sum(jnp.where(lane == r, line, 0.0), axis=-1, keepdims=True) for r in range(chip_rows)]
        came.append(decode(came_ref[:, :chip_rows, :, at].reshape(flat), jnp.concatenate(quarters, axis=0)))
    update_ref[...] = dot(came[1].astype(BF16), w_out_ref[...]).reshape(pair_ref.shape)
    d_bias = dbias_s[...]
    own = lax.rem(lanes(d_bias.shape), lanes_of_head)
    picked = [jnp.where(own == step * rows + r, d_bias, 0.0) for r in range(rows)]
    picked = jnp.concatenate(picked, axis=0)
    from_bias = jnp.zeros(flat, F32)
    for _ in range(3):
        high = picked.astype(BF16)
        from_bias = from_bias + dot(high, w_spread_ref[...])
        picked = picked - high.astype(F32)
    d_normed = came[0] + from_bias
    first_mean = jnp.mean(d_normed, axis=-1, keepdims=True)
    second_mean = jnp.mean(d_normed * normed, axis=-1, keepdims=True)
    dpair_ref[...] = (inverse * (d_normed - first_mean - normed * second_mean)).reshape(pair_ref.shape)


def shifted(array, axis, step):
    size = lax.axis_size(axis)
    return lax.ppermute(array, axis, [(s, (s + step) % size) for s in range(size)])


def kernel(fn, grid, in_specs, out_specs, out_shape, micros, name, scalars=0, scratch=(), aliases=None, vmem=24):
    return pl.pallas_call(
        fn,
        grid_spec=pltpu.PrefetchScalarGridSpec(
            num_scalar_prefetch=scalars, grid=grid, in_specs=in_specs, out_specs=out_specs, scratch_shapes=scratch
        ),
        out_shape=out_shape,
        input_output_aliases=aliases or {},
        compiler_params=pltpu.CompilerParams(vmem_limit_bytes=vmem * 1024 * 1024),
        cost_estimate=pl.CostEstimate(flops=int(micros * 1.1e9), bytes_accessed=int(micros * 2e6), transcendentals=0),
        name=name,
    )


def body(pair_act, token_mask, w_proj, w_bias, w_out, cotangent):
    rows, cells, width = pair_act.shape
    n_heads = w_bias.shape[1]
    head_dim = w_proj.shape[2] // n_heads
    my_heads = n_heads // 2
    half = my_heads * head_dim
    scale_q = 1.0 / math.sqrt(head_dim)
    nx, nyl, nz = (lax.axis_size(a) for a in ("x", "yl", "z"))
    chips = nx * nyl
    own_rows = rows // chips
    n_tokens = chips * 2 * cells
    core, z_at, yh_at = lax.axis_index("c"), lax.axis_index("z"), lax.axis_index("yh")
    cell_at = lax.axis_index(CELL)
    where = jnp.stack([core, z_at, yh_at])
    shape = jax.ShapeDtypeStruct

    def fixed(dims):
        return pl.BlockSpec(dims, lambda r, *w: (0,) * len(dims))

    def by_rows(count):
        return pl.BlockSpec((count * own_rows, cells, width), lambda r: (r, 0, 0))
    anywhere = pl.BlockSpec(memory_space=pl.ANY)

    live_here = lax.dynamic_slice_in_dim(token_mask, cell_at * cells, cells)
    live_here = jnp.broadcast_to(live_here[:, None], (cells, width))
    w_spread = jnp.repeat(w_bias, rows, axis=1)
    n_cells = chips * 2
    vmem = pl.BlockSpec(memory_space=pltpu.VMEM)
    cells_of = (2 * n_cells, cells, my_heads * rows)
    sent, bias = kernel(
        prepare_kernel, (chips // GP,),
        [by_rows(GP)] * 2 + [fixed(live_here.shape), fixed(w_spread.shape)],
        [pl.BlockSpec((GP, own_rows, cells, 2 * width), lambda r: (r, 0, 0, 0)), fixed(cells_of)],
        [shape((chips, own_rows, cells, 2 * width), BF16), shape(cells_of, F32)],
        3, "prepare",
    )(pair_act, cotangent, live_here, w_spread)

    bias = lax.all_to_all(bias, NEAR, 0, 0)
    sent = kernel(
        after_kernel, (), [anywhere, anywhere], anywhere, shape(sent.shape, sent.dtype), 0.1, "after", aliases={0: 0}
    )(sent, bias)
    block_shape = (my_heads, 2 * rows, n_tokens)
    block = kernel(
        turn_kernel, (1,), [fixed((2, n_tokens, my_heads * rows))], fixed(block_shape),
        shape(block_shape, F32), 1, "turn", scalars=1,
    )(where, bias.reshape(2, n_tokens, my_heads * rows))
    order = [0, 1, nz - 1] + list(range(2, nz - 1))
    n_now = 3
    bias_of = [block] + [shifted(block, "z", nz - s) for s in order[1:]]

    w_in, w_back, w_dm = kernel(
        functools.partial(weights_kernel, half), (1,), [fixed(w_proj.shape), fixed(w_out.shape)],
        [fixed((width, 4 * half)), fixed((4 * half, width)), fixed((width, 2 * half))],
        [shape((width, 4 * half), BF16), shape((4 * half, width), BF16), shape((width, 2 * half), BF16)],
        1, "weights", scalars=1,
    )(where, w_proj, w_out)
    live = jnp.broadcast_to(token_mask[:, None], (n_tokens, 2 * half))

    own = lax.all_to_all(sent, CHIP, 0, 0)
    own = kernel(
        after_kernel, (), [anywhere] * 5, anywhere, shape(own.shape, own.dtype), 0.1, "after_own", aliases={0: 0}
    )(own, *bias_of[1:n_now], w_in, live)
    other = shifted(own, "c", 1)

    lane_shape = (own_rows, n_tokens, 2 * half)
    n_first = n_now * 2 * rows
    first_shape = (own_rows, n_first, 2 * half)
    cell_shape = (chips, own_rows, cells, width)
    blocks = [fixed(block_shape)] * n_now
    block_out = shape(block_shape, F32)

    def of_rows(count, tokens, at=0):
        return pl.BlockSpec((count, tokens, 2 * half), lambda r, w: (r, at, 0))

    def of_cells(count, lanes_here):
        return pl.BlockSpec((chips, count, cells, lanes_here), lambda r, w: (0, r, 0, 0))

    def dkv_of(count):
        return pl.BlockSpec((count, 2 * half, n_tokens), lambda r, w: (r, 0, 0))

    qd, kv, kvm, ge, dqg, mix, dkv, *d_bias = kernel(
        functools.partial(first_kernel, half, head_dim, scale_q, order, nz, n_now), (own_rows // RA,),
        [of_cells(RA, 2 * width)] * 2 + [fixed(live.shape), fixed(w_in.shape), fixed(w_dm.shape)] + blocks,
        [of_rows(RA, n_tokens)] * 4 + [of_rows(RA, n_first)] * 2 + [dkv_of(RA)] + blocks,
        [shape(lane_shape, t) for t in (BF16, BF16, BF16, F32)]
        + [shape(first_shape, t) for t in (F32, BF16)]
        + [shape((own_rows, 2 * half, n_tokens), F32)]
        + [block_out] * n_now,
        20, "first", scalars=1, vmem=60, scratch=[pltpu.VMEM((RA, n_tokens, 2 * half), t) for t in (BF16, F32)],
    )(where, own, other, live, w_in, w_dm, *bias_of[:n_now])
    came = [shifted(d, "z", s) for d, s in zip(d_bias[1:], order[1:])]
    late_shape = block_shape[:2] + (n_tokens + 128,)
    last = of_rows(RB, n_tokens - n_first, n_now)
    keep_dn, give_dn, keep_mix, give_mix, d_late = kernel(
        functools.partial(last_kernel, half, head_dim, scale_q, order, nz), (own_rows // RB,),
        [last, of_rows(RB, n_tokens), of_rows(RB, n_tokens), last, fixed(block_shape)]
        + [of_rows(RB, n_first)] * 2 + [dkv_of(RB), fixed(w_back.shape)],
        [of_cells(RB, width)] * 4 + [fixed(late_shape)],
        [shape(cell_shape, t) for t in (F32, F32, BF16, BF16)] + [shape(late_shape, jnp.int16)],
        0.1, "last", scalars=1, vmem=60, scratch=[pltpu.VMEM(block_shape, F32)] + [pltpu.VMEM((RB, n_tokens, 2 * half), F32)] * 2,
    )(where, qd, kv, kvm, ge, bias_of[n_now], dqg, mix, dkv, w_back)

    came_late = shifted(d_late, "z", order[n_now])
    give_dn, give_mix = kernel(
        after_kernel, (), [anywhere] * 4, [anywhere] * 2,
        [shape(cell_shape, F32), shape(cell_shape, BF16)], 0.1, "after_give", aliases={0: 0, 1: 1},
    )(give_dn, give_mix, *came)
    came_dn, came_mix = shifted(give_dn, "c", 1), shifted(give_mix, "c", 1)
    cell_block = pl.BlockSpec((GM, own_rows, cells, width), lambda r: (r, 0, 0, 0))

    def wide_block(count):
        return pl.BlockSpec((count, own_rows + 1, cells, 2 * width), lambda r: (r, 0, 0, 0))

    merged = kernel(
        merge_kernel, (chips // GM,), [anywhere] + [cell_block] * 4, wide_block(GM),
        shape((chips, own_rows + 1, cells, 2 * width), jnp.int16), 2, "merge",
    )(keep_mix, keep_dn, came_dn, keep_mix, came_mix)
    back = lax.all_to_all(merged, CHIP, 0, 0)

    by_yh = (2, n_cells, cells, my_heads * rows)
    d_bias = kernel(
        turn_back_kernel, (1,), [anywhere, fixed(late_shape)] + [fixed(block_shape)] * n_now, fixed(by_yh), shape(by_yh, F32),
        1, "turn_back", scalars=1,
    )(where, back, came_late, d_bias[0], *came)
    d_bias = lax.all_to_all(d_bias.reshape(cells_of), NEAR, 0, 0)

    return kernel(
        finish_kernel, (chips // GF,),
        [by_rows(GF), wide_block(GF), fixed(cells_of), fixed(w_out.shape), fixed((n_heads * rows, width))],
        [by_rows(GF)] * 2,
        [shape(pair_act.shape, F32)] * 2,
        3, "finish", scratch=[pltpu.VMEM((cells, n_heads * rows), F32)],
    )(pair_act, back, d_bias, w_out, w_spread.T)


def solution(mesh):
    fine = Mesh(mesh.devices.reshape(4, 2, 4, 2, 2), ("z", "yh", "x", "yl", "c"))
    cells = P(("z", "yh"), CELL, None)
    return jax.shard_map(
        body,
        mesh=fine,
        in_specs=(cells, P(), P(), P(), P(), cells),
        out_specs=(cells, cells),
        check_vma=False,
    )
```

```python
import functools
import math

import jax
import jax.numpy as jnp
from jax import lax
from jax.experimental import pallas as pl
from jax.experimental.pallas import tpu as pltpu
from jax.sharding import Mesh, PartitionSpec as P

norm_eps = 1e-05
masked_score = -1000000000.0
code_top = 32000.0
RA = 2
RB = 2
GP = 4
GM = 4
GF = 4
F32 = jnp.float32
BF16 = jnp.bfloat16
CHIP = ("x", "yl")
CELL = ("x", "yl", "c")
NEAR = ("yh", "x", "yl", "c")


def dot(left, right):
    return lax.dot_general(left, right, (((1,), (0,)), ((), ())), preferred_element_type=F32)


def dot_t(left, right):
    return lax.dot_general(left, right, (((1,), (1,)), ((), ())), preferred_element_type=F32)


def dot_exact(left, right):
    high = left.astype(BF16)
    low = (left - high.astype(F32)).astype(BF16)
    return dot(high, right) + dot(low, right)


def lanes(shape):
    return lax.broadcasted_iota(jnp.int32, shape, len(shape) - 1)


def normalize(pair_act):
    average = jnp.mean(pair_act, axis=-1, keepdims=True)
    centred = pair_act - average
    spread = jnp.mean(centred * centred, axis=-1, keepdims=True)
    inverse = lax.rsqrt(spread + norm_eps)
    return (centred * inverse, inverse)


def prepare_kernel(pair_ref, cot_ref, live_ref, w_spread_ref, sent_ref, bias_ref):
    rows, cells, width = pair_ref.shape
    lanes_of_head = w_spread_ref.shape[1] // 4
    step = pl.program_id(0)
    normed_b = normalize(pair_ref[...])[0].astype(BF16)
    sent_ref[..., :width] = normed_b.reshape(sent_ref.shape[:-1] + (width,))
    sent_ref[..., width:] = cot_ref[...].reshape(sent_ref.shape[:-1] + (width,))
    spread = dot(normed_b.reshape(rows * cells, width), w_spread_ref[...]).reshape(rows, cells, -1)
    lane = lanes(spread.shape[1:])
    for c in range(2):
        half = slice(c * width, (c + 1) * width)
        total = bias_ref[c]
        for r in range(rows):
            here = lax.rem(lane[:, half], lanes_of_head) == step * rows + r
            total = jnp.where(here, jnp.where(live_ref[...] > 0, spread[r, :, half], masked_score), total)
        bias_ref[c] = total

    @pl.when(step == pl.num_programs(0) - 1)
    def _():
        for n in range(2, bias_ref.shape[0]):
            bias_ref[n] = bias_ref[n % 2]


def after_kernel(*refs):
    pass


def turn_kernel(where_ref, came_ref, out_ref):
    rows = out_ref.shape[1] // 2
    for t in range(2):
        block = came_ref[lax.rem(where_ref[2] + t, 2)].T
        for h in range(out_ref.shape[0]):
            out_ref[h, t * rows : (t + 1) * rows] = block[h * rows : (h + 1) * rows]


def turn_back_kernel(where_ref, *refs):
    here_ref, *came_refs, out_ref = refs
    total = here_ref[...]
    n_tokens = total.shape[-1]
    for ref in came_refs:
        quarters = ref[..., n_tokens:].astype(jnp.int32).astype(F32)
        total = total + decode(ref[..., :n_tokens], jnp.max(quarters, axis=-1, keepdims=True))
    rows = total.shape[1] // 2
    for t in range(2):
        both = total[:, t * rows : (t + 1) * rows].reshape(total.shape[0] * rows, -1)
        out_ref[lax.rem(where_ref[2] + t, 2)] = both.T.reshape(out_ref.shape[1:])


def weights_kernel(half, where_ref, w_proj_ref, w_out_ref, w_in_ref, w_back_ref, w_dm_ref):
    first = where_ref[0] == 0

    def mine(w):
        w = w.astype(F32)
        return jnp.where(first, w[:, :half], w[:, half:])

    w_in = jnp.concatenate([mine(w_proj_ref[n]) for n in (0, 3, 1, 2)], axis=1)
    w_in_ref[...] = w_in.astype(BF16)
    w_back_ref[...] = w_in.T.astype(BF16)
    w_dm = mine(w_out_ref[...].astype(F32).T)
    w_dm_ref[...] = jnp.concatenate([jnp.zeros_like(w_dm), w_dm], axis=1).astype(BF16)


def project(half, scale_q, first, own, other, live, w_in, w_dm):
    chips, cells, wide = own.shape
    width = wide // 2
    tokens = jnp.stack([jnp.where(first, own, other), jnp.where(first, other, own)], axis=1)
    tokens = tokens.reshape(chips * 2 * cells, wide)
    normed_b, cot = tokens[:, :width], tokens[:, width:]
    both = dot(normed_b, w_in)
    q_gate, key_value = both[:, : 2 * half], both[:, 2 * half :]
    low = lanes(q_gate.shape) < half
    gate = jax.nn.sigmoid(q_gate)
    d_att = dot(cot, w_dm) * gate
    qd = jnp.where(low, q_gate * scale_q, d_att).astype(BF16)
    kv = key_value.astype(BF16)
    kvm = jnp.where(low & (live == 0), 0.0, kv.astype(F32)).astype(BF16)
    return qd, kv, kvm, jnp.where(low, pltpu.roll(gate, half, 1), d_att)


def encode(values):
    most = jnp.maximum(jnp.max(jnp.abs(values), axis=-1, keepdims=True), 1e-30)
    quarters = jnp.floor(jnp.log(most) * (4.0 / math.log(2.0))) + 2.0
    codes = jnp.floor(values * (code_top * jnp.exp2(quarters * -0.25)) + 0.5)
    return codes.astype(jnp.int32).astype(jnp.int16), quarters


def decode(codes, quarters):
    return codes.astype(jnp.int32).astype(F32) * (jnp.exp2(quarters * 0.25) * (1.0 / code_top))


def hand_over(dbias_refs, out_refs):
    @pl.when(pl.program_id(0) == pl.num_programs(0) - 1)
    def _():
        for ref, out_ref in zip(dbias_refs, out_refs):
            n_tokens = ref.shape[-1]
            codes, quarters = encode(ref[...])
            out_ref[..., :n_tokens] = codes
            quarters = jnp.broadcast_to(quarters, codes.shape[:-1] + (out_ref.shape[-1] - n_tokens,))
            out_ref[..., n_tokens:] = quarters.astype(jnp.int32).astype(jnp.int16)


def attend(half, head_dim, scale_q, rows, bias_refs, dbias_refs):
    heads = range(half // head_dim)
    each = [(r, h) for r in range(len(rows)) for h in heads]
    block = bias_refs[0].shape[1]
    qds, ges, kvs, kvms = zip(*rows)
    lane = lanes(qds[0].shape)
    zero = jnp.zeros_like(qds[0])

    def own(h, base):
        return (lane >= base + h * head_dim) & (lane < base + (h + 1) * head_dim)

    scores = {(r, h): dot_t(jnp.where(own(h, 0), qds[r], zero), kvms[r]) for r, h in each}
    d_probs = {(r, h): dot_t(jnp.where(own(h, half), qds[r], zero), kvms[r]) for r, h in each}
    qd_t = [qd.astype(F32).T.astype(BF16) for qd in qds]
    attention, low = {}, {}
    for r, h in each:
        biased = [scores[r, h][n * block : (n + 1) * block] + ref[h] for n, ref in enumerate(bias_refs)]
        biased = jnp.concatenate(biased, axis=0)
        weights = jnp.exp(biased - jnp.max(biased, axis=-1, keepdims=True))
        attention[r, h] = weights * (1.0 / jnp.sum(weights, axis=-1, keepdims=True))
        low[r, h] = attention[r, h].astype(BF16)
    attended = [jnp.zeros(lane.shape, F32) for _ in rows]
    for r, h in each:
        attended[r] = jnp.where(own(h, half), dot(low[r, h], kvs[r]), attended[r])
    edge = [ge * att for ge, att in zip(ges, attended)]
    d_low = {}
    for h in heads:
        total = None
        for r in range(len(rows)):
            delta = jnp.sum(jnp.where(own(h, half), edge[r], 0.0), axis=-1, keepdims=True)
            d_scores = attention[r, h] * (d_probs[r, h] - delta)
            total = d_scores if total is None else total + d_scores
            d_low[r, h] = d_scores.astype(BF16)
        for n, ref in enumerate(dbias_refs):
            ref[h] += total[n * block : (n + 1) * block]
    results = []
    for r in range(len(rows)):
        gate = pltpu.roll(ges[r], half, 1)
        dqg = edge[r] * (1.0 - gate)
        for h in heads:
            dqg = jnp.where(own(h, 0), dot(d_low[r, h], kvs[r]) * scale_q, dqg)
        d_key = [dot(qd_t[r][h * head_dim : (h + 1) * head_dim], d_low[r, h]) for h in heads]
        d_value = [dot(qd_t[r][half + h * head_dim : half + (h + 1) * head_dim], low[r, h]) for h in heads]
        mixed = jnp.where(lane >= half, gate * attended[r], 0.0)
        results.append((dqg, mixed, jnp.concatenate(d_key + d_value, axis=0)))
    return results


def clear(refs):
    @pl.when(pl.program_id(0) == 0)
    def _():
        for ref in refs:
            ref[...] = jnp.zeros_like(ref)


def places(where_ref, steps, n_z, rows_j):
    at = [lax.rem(where_ref[1] + s, n_z) * 2 + lax.rem(where_ref[2] + t, 2) for s in steps for t in range(2)]
    return [pl.ds(pl.multiple_of(p * rows_j, rows_j), rows_j) for p in at]


def first_kernel(half, head_dim, scale_q, steps, n_z, n_now, where_ref, own_ref, other_ref, live_ref, w_in_ref, w_dm_ref, *refs):
    bias_refs, refs = refs[:n_now], refs[n_now:]
    (qd_ref, kv_ref, kvm_ref, ge_ref, dqg_ref, mix_ref, dkv_ref), refs = refs[:7], refs[7:]
    out_refs, (qd_s, ge_s), dbias_refs = refs[:n_now], refs[n_now : n_now + 2], refs[n_now + 2 :]
    clear(dbias_refs)
    weights = (w_in_ref[...], w_dm_ref[...])
    first = where_ref[0] == 0
    rows_j = bias_refs[0].shape[1] // 2
    now = slice(0, dqg_ref.shape[1])
    at = places(where_ref, steps, n_z, rows_j)
    rows = []
    for r in range(qd_ref.shape[0]):
        qd, kv, kvm, ge = project(half, scale_q, first, own_ref[:, r], other_ref[:, r], live_ref[...], *weights)
        kv_ref[r] = kv
        kvm_ref[r] = kvm
        qd_s[r] = qd
        ge_s[r] = ge
        for n, p in enumerate(at):
            here = slice(n * rows_j, (n + 1) * rows_j)
            qd_ref[r, here] = qd_s[r, p]
            ge_ref[r, here] = ge_s[r, p]
        rows.append((qd_ref[r, now], ge_ref[r, now], kv, kvm))
    for r, (dqg, mixed, dkv) in enumerate(attend(half, head_dim, scale_q, rows, bias_refs, dbias_refs)):
        dqg_ref[r] = dqg
        dkv_ref[r] = dkv
        mix_ref[r] = mixed.astype(BF16)
    hand_over(dbias_refs, out_refs)


def middle_kernel(half, head_dim, scale_q, where_ref, qd_ref, kv_ref, kvm_ref, ge_ref, bias_ref, dkv_in_ref, before_ref, *refs):
    dqg_ref, mix_ref, dkv_ref, out_ref, dbias_ref = refs
    clear([dbias_ref])
    rows = [(qd_ref[r], ge_ref[r], kv_ref[r], kvm_ref[r]) for r in range(qd_ref.shape[0])]
    for r, (dqg, mixed, dkv) in enumerate(attend(half, head_dim, scale_q, rows, [bias_ref], [dbias_ref])):
        dqg_ref[r] = dqg
        dkv_ref[r] = dkv_in_ref[r] + dkv
        mix_ref[r] = mixed.astype(BF16)
    hand_over([dbias_ref], [out_ref])


def last_kernel(half, head_dim, scale_q, steps, n_z, where_ref, qd_ref, kv_ref, kvm_ref, ge_ref, bias_ref, dqg_ref, mix_ref, dqg2_ref, mix2_ref, dkv_ref, w_back_ref, *refs):
    (keep_dn_ref, give_dn_ref, keep_mix_ref, give_mix_ref, dbias_ref, dn_s, mix_s) = refs
    clear([dbias_ref])
    rows = [(qd_ref[r], ge_ref[r], kv_ref[r], kvm_ref[r]) for r in range(qd_ref.shape[0])]
    results = attend(half, head_dim, scale_q, rows, [bias_ref], [dbias_ref])
    first = where_ref[0] == 0
    w_back = w_back_ref[...]
    rows_j = bias_ref.shape[1] // 2
    at = places(where_ref, steps, n_z, rows_j)
    chips, _, cells, width = keep_dn_ref.shape
    for r, (dqg, mixed, dkv) in enumerate(results):
        dn_s[r] = dot_exact((dkv + dkv_ref[r]).T, w_back[2 * half :])
        from_queries = dot_exact(jnp.concatenate([dqg_ref[r], dqg2_ref[r], dqg], axis=0), w_back[: 2 * half])
        mixed = jnp.concatenate([mix_ref[r].astype(F32), mix2_ref[r].astype(F32), mixed], axis=0)
        mixed = jnp.where(first, pltpu.roll(mixed, half, 1), mixed)
        for n, p in enumerate(at):
            here = slice(n * rows_j, (n + 1) * rows_j)
            dn_s[r, p] += from_queries[here]
            mix_s[r, p] = mixed[here]
        d_normed = dn_s[r].reshape(chips, 2, cells, width)
        mixed = mix_s[r].reshape(chips, 2, cells, width)
        keep_dn_ref[:, r] = jnp.where(first, d_normed[:, 0], d_normed[:, 1])
        give_dn_ref[:, r] = jnp.where(first, d_normed[:, 1], d_normed[:, 0])
        keep_mix_ref[:, r] = jnp.where(first, mixed[:, 0], mixed[:, 1]).astype(BF16)
        give_mix_ref[:, r] = jnp.where(first, mixed[:, 1], mixed[:, 0]).astype(BF16)


def merge_kernel(keep_dn_ref, came_dn_ref, keep_mix_ref, came_mix_ref, out_ref):
    chips, rows, cells, width = keep_dn_ref.shape
    both = (keep_dn_ref[...] + came_dn_ref[...], keep_mix_ref[...].astype(F32) + came_mix_ref[...].astype(F32))
    lane = lanes((cells, width))
    for n, values in enumerate(both):
        at = slice(n * width, (n + 1) * width)
        codes, quarters = encode(values)
        out_ref[:, :rows, :, at] = codes
        for c in range(chips):
            line = jnp.broadcast_to(quarters[c, 0], (cells, width))
            for r in range(1, rows):
                line = jnp.where(lane == r, quarters[c, r], line)
            out_ref[c, rows, :, at] = line.astype(jnp.int32).astype(jnp.int16)


def finish_kernel(pair_ref, came_ref, dbias_ref, w_out_ref, w_spread_ref, update_ref, dpair_ref, dbias_s):
    rows, cells, width = pair_ref.shape
    chips, chip_rows = came_ref.shape[0], came_ref.shape[1] - 1
    flat = (rows * cells, width)
    lanes_of_head = w_spread_ref.shape[0] // 4
    step = pl.program_id(0)

    @pl.when(step == 0)
    def _():
        for c in range(2):
            total = dbias_ref[c].astype(F32)
            for n in range(c + 2, dbias_ref.shape[0], 2):
                total = total + dbias_ref[n].astype(F32)
            dbias_s[:, c * width : (c + 1) * width] = total

    normed, inverse = normalize(pair_ref[...].reshape(flat))
    lane = lanes((cells, width))
    came = []
    for n in range(2):
        at = slice(n * width, (n + 1) * width)
        quarters = []
        for c in range(chips):
            line = came_ref[c, chip_rows, :, at].astype(jnp.int32).astype(F32)
            quarters += [jnp.sum(jnp.where(lane == r, line, 0.0), axis=-1, keepdims=True) for r in range(chip_rows)]
        came.append(decode(came_ref[:, :chip_rows, :, at].reshape(flat), jnp.concatenate(quarters, axis=0)))
    update_ref[...] = dot(came[1].astype(BF16), w_out_ref[...]).reshape(pair_ref.shape)
    d_bias = dbias_s[...]
    own = lax.rem(lanes(d_bias.shape), lanes_of_head)
    picked = [jnp.where(own == step * rows + r, d_bias, 0.0) for r in range(rows)]
    picked = jnp.concatenate(picked, axis=0)
    from_bias = jnp.zeros(flat, F32)
    for _ in range(3):
        high = picked.astype(BF16)
        from_bias = from_bias + dot(high, w_spread_ref[...])
        picked = picked - high.astype(F32)
    d_normed = came[0] + from_bias
    first_mean = jnp.mean(d_normed, axis=-1, keepdims=True)
    second_mean = jnp.mean(d_normed * normed, axis=-1, keepdims=True)
    dpair_ref[...] = (inverse * (d_normed - first_mean - normed * second_mean)).reshape(pair_ref.shape)


def shifted(array, axis, step):
    size = lax.axis_size(axis)
    return lax.ppermute(array, axis, [(s, (s + step) % size) for s in range(size)])


def kernel(fn, grid, in_specs, out_specs, out_shape, micros, name, scalars=0, scratch=(), aliases=None, vmem=24):
    return pl.pallas_call(
        fn,
        grid_spec=pltpu.PrefetchScalarGridSpec(
            num_scalar_prefetch=scalars, grid=grid, in_specs=in_specs, out_specs=out_specs, scratch_shapes=scratch
        ),
        out_shape=out_shape,
        input_output_aliases=aliases or {},
        compiler_params=pltpu.CompilerParams(vmem_limit_bytes=vmem * 1024 * 1024),
        cost_estimate=pl.CostEstimate(flops=int(micros * 1.1e9), bytes_accessed=int(micros * 2e6), transcendentals=0),
        name=name,
    )


def body(pair_act, token_mask, w_proj, w_bias, w_out, cotangent):
    rows, cells, width = pair_act.shape
    n_heads = w_bias.shape[1]
    head_dim = w_proj.shape[2] // n_heads
    my_heads = n_heads // 2
    half = my_heads * head_dim
    scale_q = 1.0 / math.sqrt(head_dim)
    nx, nyl, nz = (lax.axis_size(a) for a in ("x", "yl", "z"))
    chips = nx * nyl
    own_rows = rows // chips
    n_tokens = chips * 2 * cells
    core, z_at, yh_at = lax.axis_index("c"), lax.axis_index("z"), lax.axis_index("yh")
    cell_at = lax.axis_index(CELL)
    where = jnp.stack([core, z_at, yh_at])
    shape = jax.ShapeDtypeStruct

    def fixed(dims):
        return pl.BlockSpec(dims, lambda r, *w: (0,) * len(dims))

    def by_rows(count):
        return pl.BlockSpec((count * own_rows, cells, width), lambda r: (r, 0, 0))
    anywhere = pl.BlockSpec(memory_space=pl.ANY)

    live_here = lax.dynamic_slice_in_dim(token_mask, cell_at * cells, cells)
    live_here = jnp.broadcast_to(live_here[:, None], (cells, width))
    w_spread = jnp.repeat(w_bias, rows, axis=1)
    n_cells = chips * 2
    vmem = pl.BlockSpec(memory_space=pltpu.VMEM)
    cells_of = (2 * n_cells, cells, my_heads * rows)
    sent, bias = kernel(
        prepare_kernel, (chips // GP,),
        [by_rows(GP)] * 2 + [fixed(live_here.shape), fixed(w_spread.shape)],
        [pl.BlockSpec((GP, own_rows, cells, 2 * width), lambda r: (r, 0, 0, 0)), fixed(cells_of)],
        [shape((chips, own_rows, cells, 2 * width), BF16), shape(cells_of, F32)],
        3, "prepare",
    )(pair_act, cotangent, live_here, w_spread)

    bias = lax.all_to_all(bias, NEAR, 0, 0)
    sent = kernel(
        after_kernel, (), [anywhere, anywhere], anywhere, shape(sent.shape, sent.dtype), 0.1, "after", aliases={0: 0}
    )(sent, bias)
    block_shape = (my_heads, 2 * rows, n_tokens)
    block = kernel(
        turn_kernel, (1,), [fixed((2, n_tokens, my_heads * rows))], fixed(block_shape),
        shape(block_shape, F32), 1, "turn", scalars=1,
    )(where, bias.reshape(2, n_tokens, my_heads * rows))
    order = [1, nz - 1] + list(range(2, nz - 1)) + [0]
    n_now = 2
    bias_of = [shifted(block, "z", nz - s) for s in order[:-1]] + [block]

    w_in, w_back, w_dm = kernel(
        functools.partial(weights_kernel, half), (1,), [fixed(w_proj.shape), fixed(w_out.shape)],
        [fixed((width, 4 * half)), fixed((4 * half, width)), fixed((width, 2 * half))],
        [shape((width, 4 * half), BF16), shape((4 * half, width), BF16), shape((width, 2 * half), BF16)],
        1, "weights", scalars=1,
    )(where, w_proj, w_out)
    live = jnp.broadcast_to(token_mask[:, None], (n_tokens, 2 * half))

    own = lax.all_to_all(sent, CHIP, 0, 0)
    own = kernel(
        after_kernel, (), [anywhere] * 5, anywhere, shape(own.shape, own.dtype), 0.1, "after_own", aliases={0: 0}
    )(own, *bias_of[:n_now], w_in, live)
    other = shifted(own, "c", 1)

    lane_shape = (own_rows, n_tokens, 2 * half)
    n_first = n_now * 2 * rows
    first_shape = (own_rows, n_first, 2 * half)
    cell_shape = (chips, own_rows, cells, width)
    blocks = [fixed(block_shape)] * n_now
    block_out = shape(block_shape, F32)
    coded_shape = block_shape[:2] + (n_tokens + 128,)
    coded_out = shape(coded_shape, jnp.int16)

    def of_rows(count, tokens, at=0):
        return pl.BlockSpec((count, tokens, 2 * half), lambda r, w: (r, at, 0))

    def of_cells(count, lanes_here):
        return pl.BlockSpec((chips, count, cells, lanes_here), lambda r, w: (0, r, 0, 0))

    def dkv_of(count):
        return pl.BlockSpec((count, 2 * half, n_tokens), lambda r, w: (r, 0, 0))

    qd, kv, kvm, ge, dqg, mix, dkv, *d_bias = kernel(
        functools.partial(first_kernel, half, head_dim, scale_q, order, nz, n_now), (own_rows // RA,),
        [of_cells(RA, 2 * width)] * 2 + [fixed(live.shape), fixed(w_in.shape), fixed(w_dm.shape)] + blocks,
        [of_rows(RA, n_tokens)] * 4 + [of_rows(RA, n_first)] * 2 + [dkv_of(RA)] + [fixed(coded_shape)] * n_now,
        [shape(lane_shape, t) for t in (BF16, BF16, BF16, F32)]
        + [shape(first_shape, t) for t in (F32, BF16)]
        + [shape((own_rows, 2 * half, n_tokens), F32)]
        + [coded_out] * n_now,
        20, "first", scalars=1, vmem=60, scratch=[pltpu.VMEM((RA, n_tokens, 2 * half), t) for t in (BF16, F32)] + [pltpu.VMEM(block_shape, F32)] * n_now,
    )(where, own, other, live, w_in, w_dm, *bias_of[:n_now])
    came = [shifted(d, "z", s) for d, s in zip(d_bias, order)]
    one_block = n_tokens - n_first - 2 * rows
    middle = of_rows(RB, one_block, n_first // one_block)
    block_rows = of_rows(RB, one_block)
    block_of_rows = (own_rows, one_block, 2 * half)
    dqg2, mix2, dkv, d_far = kernel(
        functools.partial(middle_kernel, half, head_dim, scale_q), (own_rows // RB,),
        [middle, of_rows(RB, n_tokens), of_rows(RB, n_tokens), middle, fixed(block_shape), dkv_of(RB), anywhere],
        [block_rows, block_rows, dkv_of(RB), fixed(coded_shape)],
        [shape(block_of_rows, F32), shape(block_of_rows, BF16), shape(dkv.shape, F32), coded_out],
        0.1, "middle", scalars=1, vmem=60, scratch=[pltpu.VMEM(block_shape, F32)],
    )(where, qd, kv, kvm, ge, bias_of[2], dkv, kv)
    far = shifted(d_far, "z", order[2])
    last = of_rows(RB, one_block, n_first // one_block + 1)
    keep_dn, give_dn, keep_mix, give_mix, d_here = kernel(
        functools.partial(last_kernel, half, head_dim, scale_q, order, nz), (own_rows // RB,),
        [last, of_rows(RB, n_tokens), of_rows(RB, n_tokens), last, fixed(block_shape)]
        + [of_rows(RB, n_first)] * 2 + [block_rows] * 2 + [dkv_of(RB), fixed(w_back.shape)],
        [of_cells(RB, width)] * 4 + [fixed(block_shape)],
        [shape(cell_shape, t) for t in (F32, F32, BF16, BF16)] + [block_out],
        0.1, "last", scalars=1, vmem=60,
        scratch=[pltpu.VMEM((RB, n_tokens, 2 * half), F32)] * 2,
    )(where, qd, kv, kvm, ge, bias_of[3], dqg, mix, dqg2, mix2, dkv, w_back)

    by_yh = (2, n_cells, cells, my_heads * rows)
    d_bias = kernel(
        turn_back_kernel, (1,), [fixed(block_shape)] + [fixed(coded_shape)] * (nz - 1), fixed(by_yh), shape(by_yh, F32),
        1, "turn_back", scalars=1,
    )(where, d_here, *came, far)
    d_bias = lax.all_to_all(d_bias.reshape(cells_of), NEAR, 0, 0)

    give_dn, give_mix = kernel(
        after_kernel, (), [anywhere] * 5, [anywhere] * 2,
        [shape(cell_shape, F32), shape(cell_shape, BF16)], 0.1, "after_give", aliases={0: 0, 1: 1},
    )(give_dn, give_mix, far, *came)
    came_dn, came_mix = shifted(give_dn, "c", 1), shifted(give_mix, "c", 1)
    cell_block = pl.BlockSpec((GM, own_rows, cells, width), lambda r: (r, 0, 0, 0))

    def wide_block(count):
        return pl.BlockSpec((count, own_rows + 1, cells, 2 * width), lambda r: (r, 0, 0, 0))

    merged = kernel(
        merge_kernel, (chips // GM,), [cell_block] * 4, wide_block(GM),
        shape((chips, own_rows + 1, cells, 2 * width), jnp.int16), 2, "merge",
    )(keep_dn, came_dn, keep_mix, came_mix)
    merged = kernel(
        after_kernel, (), [anywhere] * 2, anywhere, shape(merged.shape, merged.dtype), 0.1, "after_merge", aliases={0: 0}
    )(merged, d_bias)
    back = lax.all_to_all(merged, CHIP, 0, 0)

    return kernel(
        finish_kernel, (chips // GF,),
        [by_rows(GF), wide_block(GF), fixed(cells_of), fixed(w_out.shape), fixed((n_heads * rows, width))],
        [by_rows(GF)] * 2,
        [shape(pair_act.shape, F32)] * 2,
        3, "finish", scratch=[pltpu.VMEM((cells, n_heads * rows), F32)],
    )(pair_act, back, d_bias, w_out, w_spread.T)


def solution(mesh):
    fine = Mesh(mesh.devices.reshape(4, 2, 4, 2, 2), ("z", "yh", "x", "yl", "c"))
    cells = P(("z", "yh"), CELL, None)
    return jax.shard_map(
        body,
        mesh=fine,
        in_specs=(cells, P(), P(), P(), P(), cells),
        out_specs=(cells, cells),
        check_vma=False,
    )
```

```python
import functools
import itertools
import math

import jax
import jax.numpy as jnp
from jax import lax
from jax.experimental import pallas as pl
from jax.experimental.pallas import tpu as pltpu
from jax.sharding import Mesh, PartitionSpec as P

norm_eps = 1e-05
masked_score = -1000000000.0
code_top = 32000.0
RA = 2
RB = 4
RL = 4
GP = 4
GM = 4
GF = 4
F32 = jnp.float32
BF16 = jnp.bfloat16
CHIP = ("x", "yl")
CELL = ("x", "yl", "c")
NEAR = ("yh", "x", "yl", "c")


def dot(left, right):
    return lax.dot_general(left, right, (((1,), (0,)), ((), ())), preferred_element_type=F32)


def dot_t(left, right):
    return lax.dot_general(left, right, (((1,), (1,)), ((), ())), preferred_element_type=F32)


def dot_exact(left, right):
    high = left.astype(BF16)
    low = (left - high.astype(F32)).astype(BF16)
    return dot(high, right) + dot(low, right)


def lanes(shape):
    return lax.broadcasted_iota(jnp.int32, shape, len(shape) - 1)


def normalize(pair_act):
    average = jnp.mean(pair_act, axis=-1, keepdims=True)
    centred = pair_act - average
    spread = jnp.mean(centred * centred, axis=-1, keepdims=True)
    inverse = lax.rsqrt(spread + norm_eps)
    return (centred * inverse, inverse)


def prepare_kernel(pair_ref, cot_ref, live_ref, w_spread_ref, sent_ref, bias_ref):
    rows, cells, width = pair_ref.shape
    lanes_of_head = w_spread_ref.shape[1] // 4
    step = pl.program_id(0)
    normed_b = normalize(pair_ref[...])[0].astype(BF16)
    sent_ref[..., :width] = normed_b.reshape(sent_ref.shape[:-1] + (width,))
    sent_ref[..., width:] = cot_ref[...].reshape(sent_ref.shape[:-1] + (width,))
    spread = dot(normed_b.reshape(rows * cells, width), w_spread_ref[...]).reshape(rows, cells, -1)
    lane = lanes(spread.shape[1:])
    for c in range(2):
        half = slice(c * width, (c + 1) * width)
        total = bias_ref[c]
        for r in range(rows):
            here = lax.rem(lane[:, half], lanes_of_head) == step * rows + r
            total = jnp.where(here, jnp.where(live_ref[...] > 0, spread[r, :, half], masked_score), total)
        bias_ref[c] = total

    @pl.when(step == pl.num_programs(0) - 1)
    def _():
        for n in range(2, bias_ref.shape[0]):
            bias_ref[n] = bias_ref[n % 2]


def after_kernel(*refs):
    pass


def turn_kernel(where_ref, came_ref, out_ref):
    rows = out_ref.shape[1] // 2
    for t in range(2):
        block = came_ref[lax.rem(where_ref[2] + t, 2)].T
        for h in range(out_ref.shape[0]):
            out_ref[h, t * rows : (t + 1) * rows] = block[h * rows : (h + 1) * rows]


def far_kernel(own_ref, *refs):
    *came_refs, out_ref = refs
    total = own_ref[...]
    for ref in came_refs:
        total = total + get_lines(ref, total.shape[-1])[:, total.shape[1] :]
    put_lines(total, out_ref)


def lines_kernel(where_ref, own_ref, *refs):
    *came_refs, keep_ref, give_ref = refs
    heads, rows, n_tokens = own_ref.shape
    chips, cells, _ = keep_ref.shape
    total = own_ref[...]
    for ref in came_refs:
        total = total + get_lines(ref, n_tokens)
    total = total.reshape(heads * rows, n_tokens).T.reshape(chips, 2, cells, heads * rows)
    first = where_ref[0] == 0
    put_lines(jnp.where(first, total[:, 0], total[:, 1]), keep_ref)
    put_lines(jnp.where(first, total[:, 1], total[:, 0]), give_ref)


def weights_kernel(half, where_ref, w_proj_ref, w_out_ref, w_in_ref, w_back_ref, w_dm_ref):
    first = where_ref[0] == 0

    def mine(w):
        w = w.astype(F32)
        return jnp.where(first, w[:, :half], w[:, half:])

    w_in = jnp.concatenate([mine(w_proj_ref[n]) for n in (0, 3, 1, 2)], axis=1)
    w_in_ref[...] = w_in.astype(BF16)
    w_back_ref[...] = w_in.T.astype(BF16)
    w_dm = mine(w_out_ref[...].astype(F32).T)
    w_dm_ref[...] = jnp.concatenate([jnp.zeros_like(w_dm), w_dm], axis=1).astype(BF16)


def project(half, scale_q, first, own, other, live, w_in, w_dm):
    chips, cells, wide = own.shape
    width = wide // 2
    tokens = jnp.stack([jnp.where(first, own, other), jnp.where(first, other, own)], axis=1)
    tokens = tokens.reshape(chips * 2 * cells, wide)
    normed_b, cot = tokens[:, :width], tokens[:, width:]
    both = dot(normed_b, w_in)
    q_gate, key_value = both[:, : 2 * half], both[:, 2 * half :]
    low = lanes(q_gate.shape) < half
    gate = jax.nn.sigmoid(q_gate)
    d_att = dot(cot, w_dm) * gate
    qd = jnp.where(low, q_gate * scale_q, d_att).astype(BF16)
    kv = key_value.astype(BF16)
    kvm = jnp.where(low & (live == 0), 0.0, kv.astype(F32)).astype(BF16)
    return qd, kv, kvm, jnp.where(low, pltpu.roll(gate, half, 1), d_att)


def exponents(most):
    return jnp.floor(jnp.log(jnp.maximum(most, 1e-30)) * (4.0 / math.log(2.0))) + 2.0


def encode(values, quarters):
    codes = jnp.floor(values * (code_top * jnp.exp2(quarters * -0.25)) + 0.5)
    return codes.astype(jnp.int32)


def decode(codes, quarters):
    return codes.astype(jnp.int32).astype(F32) * (jnp.exp2(quarters * 0.25) * (1.0 / code_top))


def put_lines(values, out_ref):
    size = values.shape[-1]
    quarters = exponents(jnp.max(jnp.abs(values), axis=-1, keepdims=True))
    out_ref[..., :size] = encode(values, quarters).astype(jnp.int16)
    quarters = jnp.broadcast_to(quarters, values.shape[:-1] + (out_ref.shape[-1] - size,))
    out_ref[..., size:] = quarters.astype(jnp.int32).astype(jnp.int16)


def get_lines(ref, size):
    quarters = ref[..., size:].astype(jnp.int32).astype(F32)
    return decode(ref[..., :size], jnp.max(quarters, axis=-1, keepdims=True))


def hand_over(dbias_refs, out_refs):
    @pl.when(pl.program_id(0) == pl.num_programs(0) - 1)
    def _():
        for ref, out_ref in zip(dbias_refs, out_refs):
            put_lines(ref[...], out_ref)


def attend(half, head_dim, scale_q, rows, bias_refs, dbias_refs):
    heads = range(half // head_dim)
    each = [(r, h) for r in range(len(rows)) for h in heads]
    ends = list(itertools.accumulate(ref.shape[1] for ref in bias_refs))
    cuts = [slice(end - ref.shape[1], end) for end, ref in zip(ends, bias_refs)]
    qds, ges, kvs, kvms = zip(*rows)
    lane = lanes(qds[0].shape)
    zero = jnp.zeros_like(qds[0])

    def own(h, base):
        return (lane >= base + h * head_dim) & (lane < base + (h + 1) * head_dim)

    scores = {(r, h): dot_t(jnp.where(own(h, 0), qds[r], zero), kvms[r]) for r, h in each}
    d_probs = {(r, h): dot_t(jnp.where(own(h, half), qds[r], zero), kvms[r]) for r, h in each}
    qd_t = [qd.astype(F32).T.astype(BF16) for qd in qds]
    attention, low = {}, {}
    for r, h in each:
        biased = [scores[r, h][cut] + ref[h] for cut, ref in zip(cuts, bias_refs)]
        biased = jnp.concatenate(biased, axis=0)
        weights = jnp.exp(biased - jnp.max(biased, axis=-1, keepdims=True))
        attention[r, h] = weights * (1.0 / jnp.sum(weights, axis=-1, keepdims=True))
        low[r, h] = attention[r, h].astype(BF16)
    attended = [jnp.zeros(lane.shape, F32) for _ in rows]
    for r, h in each:
        attended[r] = jnp.where(own(h, half), dot(low[r, h], kvs[r]), attended[r])
    edge = [ge * att for ge, att in zip(ges, attended)]
    d_low = {}
    for h in heads:
        total = None
        for r in range(len(rows)):
            delta = jnp.sum(jnp.where(own(h, half), edge[r], 0.0), axis=-1, keepdims=True)
            d_scores = attention[r, h] * (d_probs[r, h] - delta)
            total = d_scores if total is None else total + d_scores
            d_low[r, h] = d_scores.astype(BF16)
        for cut, ref in zip(cuts, dbias_refs):
            ref[h] += total[cut]
    results = []
    for r in range(len(rows)):
        gate = pltpu.roll(ges[r], half, 1)
        dqg = edge[r] * (1.0 - gate)
        for h in heads:
            dqg = jnp.where(own(h, 0), dot(d_low[r, h], kvs[r]) * scale_q, dqg)
        d_key = [dot(qd_t[r][h * head_dim : (h + 1) * head_dim], d_low[r, h]) for h in heads]
        d_value = [dot(qd_t[r][half + h * head_dim : half + (h + 1) * head_dim], low[r, h]) for h in heads]
        mixed = jnp.where(lane >= half, gate * attended[r], 0.0)
        results.append((dqg, mixed, jnp.concatenate(d_key + d_value, axis=0)))
    return results


def clear(refs):
    @pl.when(pl.program_id(0) == 0)
    def _():
        for ref in refs:
            ref[...] = jnp.zeros_like(ref)


def places(where_ref, order, n_z, rows_j):
    at = [lax.rem(where_ref[1] + s, n_z) * 2 + lax.rem(where_ref[2] + t, 2) for s, t in order]
    return [pl.ds(pl.multiple_of(p * rows_j, rows_j), rows_j) for p in at]


def first_kernel(half, head_dim, scale_q, order, n_z, n_now, where_ref, own_ref, other_ref, live_ref, w_in_ref, w_dm_ref, *refs):
    bias_refs, refs = refs[:n_now], refs[n_now:]
    (qd_ref, kv_ref, kvm_ref, ge_ref, dqg_ref, mix_ref, dkv_ref), refs = refs[:7], refs[7:]
    out_refs, (qd_s, ge_s), dbias_refs = refs[:n_now], refs[n_now : n_now + 2], refs[n_now + 2 :]
    clear(dbias_refs)
    weights = (w_in_ref[...], w_dm_ref[...])
    first = where_ref[0] == 0
    rows_j = bias_refs[0].shape[1] // 2
    now = slice(0, dqg_ref.shape[1])
    at = places(where_ref, order, n_z, rows_j)
    rows = []
    for r in range(qd_ref.shape[0]):
        qd, kv, kvm, ge = project(half, scale_q, first, own_ref[:, r], other_ref[:, r], live_ref[...], *weights)
        kv_ref[r] = kv
        kvm_ref[r] = kvm
        qd_s[r] = qd
        ge_s[r] = ge
        for n, p in enumerate(at):
            here = slice(n * rows_j, (n + 1) * rows_j)
            qd_ref[r, here] = qd_s[r, p]
            ge_ref[r, here] = ge_s[r, p]
        rows.append((qd_ref[r, now], ge_ref[r, now], kv, kvm))
    for r, (dqg, mixed, dkv) in enumerate(attend(half, head_dim, scale_q, rows, bias_refs, dbias_refs)):
        dqg_ref[r] = dqg
        dkv_ref[r] = dkv
        mix_ref[r] = mixed.astype(BF16)
    hand_over(dbias_refs, out_refs)


def middle_kernel(half, head_dim, scale_q, at, where_ref, qd_ref, kv_ref, kvm_ref, ge_ref, far_bias_ref, own_bias_ref, dkv_in_ref, *refs):
    dqg_ref, mix_ref, dkv_ref, near_ref, far_ref, own_ref, dbias_ref = refs
    clear([dbias_ref, own_ref])
    rows = [(qd_ref[r, at], ge_ref[r, at], kv_ref[r], kvm_ref[r]) for r in range(qd_ref.shape[0])]
    results = attend(half, head_dim, scale_q, rows, [far_bias_ref, own_bias_ref], [dbias_ref, own_ref])
    for r, (dqg, mixed, dkv) in enumerate(results):
        dqg_ref[r] = dqg
        dkv_ref[r] = dkv_in_ref[r] + dkv
        mix_ref[r] = mixed.astype(BF16)

    @pl.when(pl.program_id(0) == pl.num_programs(0) - 1)
    def _():
        rows_j = near_ref.shape[1]
        put_lines(dbias_ref[:, :rows_j], near_ref)
        put_lines(dbias_ref[:, rows_j:], far_ref)


def last_kernel(half, head_dim, scale_q, order, n_z, where_ref, qd_ref, kv_ref, kvm_ref, ge_ref, bias_ref, dqg_ref, mix_ref, dqg2_ref, mix2_ref, dkv_ref, w_back_ref, *refs):
    (keep_dn_ref, give_dn_ref, keep_mix_ref, give_mix_ref, dbias_ref, dn_s, mix_s) = refs
    clear([dbias_ref])
    rows = [(qd_ref[r], ge_ref[r], kv_ref[r], kvm_ref[r]) for r in range(qd_ref.shape[0])]
    results = attend(half, head_dim, scale_q, rows, [bias_ref], [dbias_ref])
    first = where_ref[0] == 0
    w_back = w_back_ref[...]
    rows_j = bias_ref.shape[1]
    at = places(where_ref, order, n_z, rows_j)
    chips, _, cells, width = keep_dn_ref.shape
    for r, (dqg, mixed, dkv) in enumerate(results):
        dn_s[r] = dot_exact((dkv + dkv_ref[r]).T, w_back[2 * half :])
        from_queries = dot_exact(jnp.concatenate([dqg_ref[r], dqg2_ref[r], dqg], axis=0), w_back[: 2 * half])
        mixed = jnp.concatenate([mix_ref[r].astype(F32), mix2_ref[r].astype(F32), mixed], axis=0)
        mixed = jnp.where(first, pltpu.roll(mixed, half, 1), mixed)
        for n, p in enumerate(at):
            here = slice(n * rows_j, (n + 1) * rows_j)
            dn_s[r, p] += from_queries[here]
            mix_s[r, p] = mixed[here]
        d_normed = dn_s[r].reshape(chips, 2, cells, width)
        mixed = mix_s[r].reshape(chips, 2, cells, width)
        keep_dn_ref[:, r] = jnp.where(first, d_normed[:, 0], d_normed[:, 1])
        give_dn_ref[:, r] = jnp.where(first, d_normed[:, 1], d_normed[:, 0])
        keep_mix_ref[:, r] = jnp.where(first, mixed[:, 0], mixed[:, 1]).astype(BF16)
        give_mix_ref[:, r] = jnp.where(first, mixed[:, 1], mixed[:, 0]).astype(BF16)


def merge_kernel(where_ref, keep_dn_ref, came_dn_ref, keep_mix_ref, came_mix_ref, keep_lines_ref, came_lines_ref, out_ref):
    chips, rows, cells, width = keep_dn_ref.shape
    d_normed = keep_dn_ref[...] + came_dn_ref[...]
    d_normed = d_normed - d_normed[..., width - 1 :]
    mixed = keep_mix_ref[...].astype(F32) + came_mix_ref[...].astype(F32)
    first = where_ref[0] == 0
    keep, came = (ref[...].astype(jnp.int32) for ref in (keep_lines_ref, came_lines_ref))
    lines = (jnp.where(first, keep, came), jnp.where(first, came, keep))
    lane = lanes((cells, width))
    for c in range(chips):
        scales = []
        for values in (d_normed, mixed):
            most = jnp.max(jnp.max(jnp.abs(values[c]), axis=0), axis=-1, keepdims=True)
            scales.append(jnp.broadcast_to(exponents(most), (cells, width)))
        slots = [s.astype(jnp.int32) for s in scales] + [line[c, :, width:] for line in lines]
        for r in range(rows):
            codes = encode(d_normed[c, r], scales[0])
            if r < len(slots):
                codes = jnp.where(lane == width - 1, slots[r], codes)
            out_ref[c, r, :, :width] = codes.astype(jnp.int16)
            out_ref[c, r, :, width:] = encode(mixed[c, r], scales[1]).astype(jnp.int16)
        for n in range(2):
            out_ref[c, rows, :, n * width : (n + 1) * width] = lines[n][c, :, :width].astype(jnp.int16)


def finish_kernel(pair_ref, came_ref, scales_ref, lines_ref, w_out_ref, w_spread_ref, update_ref, dpair_ref, dbias_s):
    rows, cells, width = pair_ref.shape
    chips, chip_rows = came_ref.shape[0], came_ref.shape[1] - 1
    flat = (rows * cells, width)
    lanes_of_head = w_spread_ref.shape[0] // 4
    step = pl.program_id(0)
    last = lanes((cells, width)) == width - 1

    def slot(line):
        line = line.astype(jnp.int32).astype(F32)
        return jnp.sum(jnp.where(last, line, 0.0), axis=-1, keepdims=True)

    @pl.when(step == 0)
    def _():
        for c in range(2):
            at = slice(c * width, (c + 1) * width)
            total = jnp.zeros((cells, width), F32)
            for n in range(lines_ref.shape[0]):
                total = total + decode(lines_ref[n, 0, :, at], slot(scales_ref[n, c, :, :width]))
            dbias_s[:, c * width : (c + 1) * width] = total

    normed, inverse = normalize(pair_ref[...].reshape(flat))
    came = []
    for n in range(2):
        parts = []
        for c in range(chips):
            scale = slot(came_ref[c, n, :, :width])
            for r in range(chip_rows):
                part = decode(came_ref[c, r, :, n * width : (n + 1) * width], scale)
                parts.append(jnp.where(last, 0.0, part) if n == 0 else part)
        came.append(jnp.concatenate(parts, axis=0))
    update_ref[...] = dot(came[1].astype(BF16), w_out_ref[...]).reshape(pair_ref.shape)
    d_bias = dbias_s[...]
    own = lax.rem(lanes(d_bias.shape), lanes_of_head)
    picked = [jnp.where(own == step * rows + r, d_bias, 0.0) for r in range(rows)]
    picked = jnp.concatenate(picked, axis=0)
    from_bias = jnp.zeros(flat, F32)
    for _ in range(3):
        high = picked.astype(BF16)
        from_bias = from_bias + dot(high, w_spread_ref[...])
        picked = picked - high.astype(F32)
    d_normed = came[0] + from_bias
    first_mean = jnp.mean(d_normed, axis=-1, keepdims=True)
    second_mean = jnp.mean(d_normed * normed, axis=-1, keepdims=True)
    dpair_ref[...] = (inverse * (d_normed - first_mean - normed * second_mean)).reshape(pair_ref.shape)


def shifted(array, axis, step):
    size = lax.axis_size(axis)
    return lax.ppermute(array, axis, [(s, (s + step) % size) for s in range(size)])


def kernel(fn, grid, in_specs, out_specs, out_shape, micros, name, scalars=0, scratch=(), aliases=None, vmem=24):
    return pl.pallas_call(
        fn,
        grid_spec=pltpu.PrefetchScalarGridSpec(
            num_scalar_prefetch=scalars, grid=grid, in_specs=in_specs, out_specs=out_specs, scratch_shapes=scratch
        ),
        out_shape=out_shape,
        input_output_aliases=aliases or {},
        compiler_params=pltpu.CompilerParams(vmem_limit_bytes=vmem * 1024 * 1024),
        cost_estimate=pl.CostEstimate(flops=int(micros * 1.1e9), bytes_accessed=int(micros * 2e6), transcendentals=0),
        name=name,
    )


def body(pair_act, token_mask, w_proj, w_bias, w_out, cotangent):
    rows, cells, width = pair_act.shape
    n_heads = w_bias.shape[1]
    head_dim = w_proj.shape[2] // n_heads
    my_heads = n_heads // 2
    half = my_heads * head_dim
    scale_q = 1.0 / math.sqrt(head_dim)
    nx, nyl, nz = (lax.axis_size(a) for a in ("x", "yl", "z"))
    chips = nx * nyl
    own_rows = rows // chips
    n_tokens = chips * 2 * cells
    core, z_at, yh_at = lax.axis_index("c"), lax.axis_index("z"), lax.axis_index("yh")
    cell_at = lax.axis_index(CELL)
    where = jnp.stack([core, z_at, yh_at])
    shape = jax.ShapeDtypeStruct

    def fixed(dims):
        return pl.BlockSpec(dims, lambda r, *w: (0,) * len(dims))

    def by_rows(count):
        return pl.BlockSpec((count * own_rows, cells, width), lambda r: (r, 0, 0))
    anywhere = pl.BlockSpec(memory_space=pl.ANY)

    live_here = lax.dynamic_slice_in_dim(token_mask, cell_at * cells, cells)
    live_here = jnp.broadcast_to(live_here[:, None], (cells, width))
    w_spread = jnp.repeat(w_bias, rows, axis=1)
    n_cells = chips * 2
    vmem = pl.BlockSpec(memory_space=pltpu.VMEM)
    cells_of = (2 * n_cells, cells, my_heads * rows)
    sent, bias = kernel(
        prepare_kernel, (chips // GP,),
        [by_rows(GP)] * 2 + [fixed(live_here.shape), fixed(w_spread.shape)],
        [pl.BlockSpec((GP, own_rows, cells, 2 * width), lambda r: (r, 0, 0, 0)), fixed(cells_of)],
        [shape((chips, own_rows, cells, 2 * width), BF16), shape(cells_of, F32)],
        3, "prepare",
    )(pair_act, cotangent, live_here, w_spread)

    bias = lax.all_to_all(bias, NEAR, 0, 0)
    sent = kernel(
        after_kernel, (), [anywhere, anywhere], anywhere, shape(sent.shape, sent.dtype), 0.1, "after", aliases={0: 0}
    )(sent, bias)
    block_shape = (my_heads, 2 * rows, n_tokens)
    block = kernel(
        turn_kernel, (1,), [fixed((2, n_tokens, my_heads * rows))], fixed(block_shape),
        shape(block_shape, F32), 1, "turn", scalars=1,
    )(where, bias.reshape(2, n_tokens, my_heads * rows))
    order = [(1, 0), (1, 1), (nz - 1, 0), (nz - 1, 1), (2, 0), (2, 1), (0, 1), (0, 0)]
    n_now = 2
    after_it = shifted(block, "z", 1)
    before_it = shifted(block, "z", nz - 1)
    bias_of = [before_it, after_it, shifted(block, "z", nz - 2)]

    w_in, w_back, w_dm = kernel(
        functools.partial(weights_kernel, half), (1,), [fixed(w_proj.shape), fixed(w_out.shape)],
        [fixed((width, 4 * half)), fixed((4 * half, width)), fixed((width, 2 * half))],
        [shape((width, 4 * half), BF16), shape((4 * half, width), BF16), shape((width, 2 * half), BF16)],
        1, "weights", scalars=1,
    )(where, w_proj, w_out)
    live = jnp.broadcast_to(token_mask[:, None], (n_tokens, 2 * half))

    own = lax.all_to_all(sent, CHIP, 0, 0)
    own = kernel(
        after_kernel, (), [anywhere] * 5, anywhere, shape(own.shape, own.dtype), 0.1, "after_own", aliases={0: 0}
    )(own, bias_of[1], bias_of[0], w_in, live)
    other = shifted(own, "c", 1)

    lane_shape = (own_rows, n_tokens, 2 * half)
    n_first = n_now * 2 * rows
    first_shape = (own_rows, n_first, 2 * half)
    cell_shape = (chips, own_rows, cells, width)
    blocks = [fixed(block_shape)] * n_now
    block_out = shape(block_shape, F32)
    coded_shape = block_shape[:2] + (n_tokens + 128,)
    coded_out = shape(coded_shape, jnp.int16)

    def of_rows(count, tokens, at=0):
        return pl.BlockSpec((count, tokens, 2 * half), lambda r, w: (r, at, 0))

    def of_cells(count, lanes_here):
        return pl.BlockSpec((chips, count, cells, lanes_here), lambda r, w: (0, r, 0, 0))

    def dkv_of(count):
        return pl.BlockSpec((count, 2 * half, n_tokens), lambda r, w: (r, 0, 0))

    qd, kv, kvm, ge, dqg, mix, dkv, *d_bias = kernel(
        functools.partial(first_kernel, half, head_dim, scale_q, order, nz, n_now), (own_rows // RA,),
        [of_cells(RA, 2 * width)] * 2 + [fixed(live.shape), fixed(w_in.shape), fixed(w_dm.shape)] + blocks,
        [of_rows(RA, n_tokens)] * 4 + [of_rows(RA, n_first)] * 2 + [dkv_of(RA)] + [fixed(coded_shape)] * n_now,
        [shape(lane_shape, t) for t in (BF16, BF16, BF16, F32)]
        + [shape(first_shape, t) for t in (F32, BF16)]
        + [shape((own_rows, 2 * half, n_tokens), F32)]
        + [coded_out] * n_now,
        20, "first", scalars=1, vmem=60, scratch=[pltpu.VMEM((RA, n_tokens, 2 * half), t) for t in (BF16, F32)] + [pltpu.VMEM(block_shape, F32)] * n_now,
    )(where, own, other, live, w_in, w_dm, *bias_of[:n_now])
    came = [shifted(d, "z", s) for d, s in zip(d_bias, (1, nz - 1))]
    n_middle = 3 * rows
    middle_rows = of_rows(RB, n_middle)
    middle_shape = (own_rows, n_middle, 2 * half)
    half_shape = (my_heads, rows, n_tokens)
    lines_out = (my_heads, rows, n_tokens + 128)
    near_half = pl.BlockSpec(half_shape, lambda r, w: (0, 0, 0))
    far_half = pl.BlockSpec(half_shape, lambda r, w: (0, 1, 0))
    whole_row = of_rows(RB, n_tokens)
    dqg2, mix2, dkv, d_near, d_far, d_own = kernel(
        functools.partial(middle_kernel, half, head_dim, scale_q, slice(n_first, n_first + n_middle)), (own_rows // RB,),
        [whole_row] * 4 + [fixed(block_shape), far_half, dkv_of(RB)],
        [middle_rows, middle_rows, dkv_of(RB), fixed(lines_out), fixed(lines_out), fixed(half_shape)],
        [shape(middle_shape, F32), shape(middle_shape, BF16), shape(dkv.shape, F32)]
        + [shape(lines_out, jnp.int16)] * 2 + [shape(half_shape, F32)],
        0.1, "middle", scalars=1, vmem=60, scratch=[pltpu.VMEM(block_shape, F32)],
    )(where, qd, kv, kvm, ge, bias_of[2], block, dkv)
    across = [(s, (s // 2 + 2) % nz * 2 + 1 - s % 2) for s in range(2 * nz)]
    came_near, came_far = shifted(d_near, "z", 2), lax.ppermute(d_far, ("z", "yh"), across)
    d_own = kernel(
        far_kernel, (1,), [fixed(half_shape)] + [fixed(coded_shape)] * 2, fixed(lines_out), shape(lines_out, jnp.int16),
        0.1, "far",
    )(d_own, *came)
    came_own = shifted(d_own, "yh", 1)
    last = of_rows(RL, rows, n_tokens // rows - 1)
    keep_dn, give_dn, keep_mix, give_mix, d_here = kernel(
        functools.partial(last_kernel, half, head_dim, scale_q, order, nz), (own_rows // RL,),
        [last, of_rows(RL, n_tokens), of_rows(RL, n_tokens), last, near_half]
        + [of_rows(RL, n_first)] * 2 + [of_rows(RL, n_middle)] * 2 + [dkv_of(RL), fixed(w_back.shape)],
        [of_cells(RL, width)] * 4 + [fixed(half_shape)],
        [shape(cell_shape, t) for t in (F32, F32, BF16, BF16)] + [shape(half_shape, F32)],
        0.1, "last", scalars=1, vmem=60,
        scratch=[pltpu.VMEM((RL, n_tokens, 2 * half), F32)] * 2,
    )(where, qd, kv, kvm, ge, block, dqg, mix, dqg2, mix2, dkv, w_back)

    lines_shape = (chips, cells, 2 * width)
    keep_lines, give_lines = kernel(
        lines_kernel, (1,), [fixed(half_shape)] + [fixed(lines_out)] * 5, [fixed(lines_shape)] * 2,
        [shape(lines_shape, jnp.int16)] * 2, 1, "lines", scalars=1,
    )(where, d_here, *came, came_near, came_far, came_own)
    came_lines = shifted(give_lines, "c", 1)

    give_dn, give_mix = kernel(
        after_kernel, (), [anywhere] * 5, [anywhere] * 2,
        [shape(cell_shape, F32), shape(cell_shape, BF16)], 0.1, "after_give", aliases={0: 0, 1: 1},
    )(give_dn, give_mix, came_near, came_far, came_own)
    came_dn, came_mix = shifted(give_dn, "c", 1), shifted(give_mix, "c", 1)
    cell_block = pl.BlockSpec((GM, own_rows, cells, width), lambda r, w: (r, 0, 0, 0))
    line_block = pl.BlockSpec((GM, cells, 2 * width), lambda r, w: (r, 0, 0))

    def wide_block(count):
        return pl.BlockSpec((count, own_rows + 1, cells, 2 * width), lambda r, *w: (r, 0, 0, 0))

    merged = kernel(
        merge_kernel, (chips // GM,), [cell_block] * 4 + [line_block] * 2, wide_block(GM),
        shape((chips, own_rows + 1, cells, 2 * width), jnp.int16), 2, "merge", scalars=1,
    )(where, keep_dn, came_dn, keep_mix, came_mix, keep_lines, came_lines)
    back = lax.all_to_all(merged, CHIP, 0, 0)

    def rows_of(count, at):
        return pl.BlockSpec((chips, count, cells, 2 * width), lambda r: (0, at, 0, 0))

    return kernel(
        finish_kernel, (chips // GF,),
        [by_rows(GF), wide_block(GF), rows_of(2, 1), rows_of(1, own_rows), fixed(w_out.shape), fixed((n_heads * rows, width))],
        [by_rows(GF)] * 2,
        [shape(pair_act.shape, F32)] * 2,
        3, "finish", scratch=[pltpu.VMEM((cells, n_heads * rows), F32)],
    )(pair_act, back, back, back, w_out, w_spread.T)


def solution(mesh):
    fine = Mesh(mesh.devices.reshape(4, 2, 4, 2, 2), ("z", "yh", "x", "yl", "c"))
    cells = P(("z", "yh"), CELL, None)
    return jax.shard_map(
        body,
        mesh=fine,
        in_specs=(cells, P(), P(), P(), P(), cells),
        out_specs=(cells, cells),
        check_vma=False,
    )
```

```python
import functools
import itertools
import math

import jax
import jax.numpy as jnp
from jax import lax
from jax.experimental import pallas as pl
from jax.experimental.pallas import tpu as pltpu
from jax.sharding import Mesh, PartitionSpec as P

norm_eps = 1e-05
masked_score = -1000000000.0
code_top = 32000.0
RA = 2
RB = 2
RL = 4
GP = 8
GM = 8
GF = 8
F32 = jnp.float32
BF16 = jnp.bfloat16
CHIP = ("x", "yl")
CELL = ("x", "yl", "c")
NEAR = ("yh", "x", "yl", "c")


def dot(left, right):
    return lax.dot_general(left, right, (((1,), (0,)), ((), ())), preferred_element_type=F32)


def dot_t(left, right):
    return lax.dot_general(left, right, (((1,), (1,)), ((), ())), preferred_element_type=F32)


def dot_exact(left, right):
    high = left.astype(BF16)
    low = (left - high.astype(F32)).astype(BF16)
    return dot(high, right) + dot(low, right)


def lanes(shape):
    return lax.broadcasted_iota(jnp.int32, shape, len(shape) - 1)


def normalize(pair_act):
    average = jnp.mean(pair_act, axis=-1, keepdims=True)
    centred = pair_act - average
    spread = jnp.mean(centred * centred, axis=-1, keepdims=True)
    inverse = lax.rsqrt(spread + norm_eps)
    return (centred * inverse, inverse)


def prepare_kernel(pair_ref, cot_ref, live_ref, w_spread_ref, sent_ref, bias_ref):
    rows, cells, width = pair_ref.shape
    lanes_of_head = w_spread_ref.shape[1] // 4
    step = pl.program_id(0)
    normed_b = normalize(pair_ref[...])[0].astype(BF16)
    sent_ref[..., :width] = normed_b.reshape(sent_ref.shape[:-1] + (width,))
    sent_ref[..., width:] = cot_ref[...].reshape(sent_ref.shape[:-1] + (width,))
    spread = dot(normed_b.reshape(rows * cells, width), w_spread_ref[...]).reshape(rows, cells, -1)
    lane = lanes(spread.shape[1:])
    for c in range(2):
        half = slice(c * width, (c + 1) * width)
        total = bias_ref[c]
        for r in range(rows):
            here = lax.rem(lane[:, half], lanes_of_head) == step * rows + r
            total = jnp.where(here, jnp.where(live_ref[...] > 0, spread[r, :, half], masked_score), total)
        bias_ref[c] = total

    @pl.when(step == pl.num_programs(0) - 1)
    def _():
        for n in range(2, bias_ref.shape[0]):
            bias_ref[n] = bias_ref[n % 2]


def after_kernel(*refs):
    pass


def turn_kernel(where_ref, came_ref, out_ref):
    rows = out_ref.shape[1] // 2
    for t in range(2):
        block = came_ref[lax.rem(where_ref[2] + t, 2)].T
        for h in range(out_ref.shape[0]):
            out_ref[h, t * rows : (t + 1) * rows] = block[h * rows : (h + 1) * rows]


def far_kernel(own_ref, *refs):
    *came_refs, out_ref = refs
    total = own_ref[...]
    for ref in came_refs:
        total = total + get_lines(ref, total.shape[-1])[:, total.shape[1] :]
    put_lines(total, out_ref)


def lines_kernel(where_ref, own_ref, *refs):
    *came_refs, keep_ref, give_ref = refs
    heads, rows, n_tokens = own_ref.shape
    chips, cells, _ = keep_ref.shape
    total = own_ref[...]
    for ref in came_refs:
        total = total + get_lines(ref, n_tokens)
    total = total.reshape(heads * rows, n_tokens).T.reshape(chips, 2, cells, heads * rows)
    first = where_ref[0] == 0
    put_lines(jnp.where(first, total[:, 0], total[:, 1]), keep_ref)
    put_lines(jnp.where(first, total[:, 1], total[:, 0]), give_ref)


def weights_kernel(half, where_ref, w_proj_ref, w_out_ref, w_in_ref, w_back_ref, w_dm_ref):
    first = where_ref[0] == 0

    def mine(w):
        w = w.astype(F32)
        return jnp.where(first, w[:, :half], w[:, half:])

    w_in = jnp.concatenate([mine(w_proj_ref[n]) for n in (0, 3, 1, 2)], axis=1)
    w_in_ref[...] = w_in.astype(BF16)
    w_back_ref[...] = w_in.T.astype(BF16)
    w_dm = mine(w_out_ref[...].astype(F32).T)
    w_dm_ref[...] = jnp.concatenate([jnp.zeros_like(w_dm), w_dm], axis=1).astype(BF16)


def project(half, scale_q, first, own, other, live, w_in, w_dm):
    chips, cells, wide = own.shape
    width = wide // 2
    tokens = jnp.stack([jnp.where(first, own, other), jnp.where(first, other, own)], axis=1)
    tokens = tokens.reshape(chips * 2 * cells, wide)
    normed_b, cot = tokens[:, :width], tokens[:, width:]
    both = dot(normed_b, w_in)
    q_gate, key_value = both[:, : 2 * half], both[:, 2 * half :]
    low = lanes(q_gate.shape) < half
    gate = jax.nn.sigmoid(q_gate)
    d_att = dot(cot, w_dm) * gate
    qd = jnp.where(low, q_gate * scale_q, d_att).astype(BF16)
    kv = key_value.astype(BF16)
    kvm = jnp.where(low & (live == 0), 0.0, kv.astype(F32)).astype(BF16)
    return qd, kv, kvm, jnp.where(low, pltpu.roll(gate, half, 1), d_att)


def exponents(most):
    return jnp.floor(jnp.log(jnp.maximum(most, 1e-30)) * (4.0 / math.log(2.0))) + 2.0


def encode(values, quarters):
    codes = jnp.floor(values * (code_top * jnp.exp2(quarters * -0.25)) + 0.5)
    return codes.astype(jnp.int32)


def decode(codes, quarters):
    return codes.astype(jnp.int32).astype(F32) * (jnp.exp2(quarters * 0.25) * (1.0 / code_top))


def put_lines(values, out_ref):
    size = values.shape[-1]
    quarters = exponents(jnp.max(jnp.abs(values), axis=-1, keepdims=True))
    out_ref[..., :size] = encode(values, quarters).astype(jnp.int16)
    quarters = jnp.broadcast_to(quarters, values.shape[:-1] + (out_ref.shape[-1] - size,))
    out_ref[..., size:] = quarters.astype(jnp.int32).astype(jnp.int16)


def get_lines(ref, size):
    quarters = ref[..., size:].astype(jnp.int32).astype(F32)
    return decode(ref[..., :size], jnp.max(quarters, axis=-1, keepdims=True))


def hand_over(dbias_refs, out_refs):
    @pl.when(pl.program_id(0) == pl.num_programs(0) - 1)
    def _():
        for ref, out_ref in zip(dbias_refs, out_refs):
            put_lines(ref[...], out_ref)


def attend(half, head_dim, scale_q, rows, bias_refs, dbias_refs):
    heads = range(half // head_dim)
    each = [(r, h) for r in range(len(rows)) for h in heads]
    ends = list(itertools.accumulate(ref.shape[1] for ref in bias_refs))
    cuts = [slice(end - ref.shape[1], end) for end, ref in zip(ends, bias_refs)]
    qds, ges, kvs, kvms = zip(*rows)
    lane = lanes(qds[0].shape)
    zero = jnp.zeros_like(qds[0])

    def own(h, base):
        return (lane >= base + h * head_dim) & (lane < base + (h + 1) * head_dim)

    scores = {(r, h): dot_t(jnp.where(own(h, 0), qds[r], zero), kvms[r]) for r, h in each}
    d_probs = {(r, h): dot_t(jnp.where(own(h, half), qds[r], zero), kvms[r]) for r, h in each}
    qd_t = [qd.astype(F32).T.astype(BF16) for qd in qds]
    attention, low = {}, {}
    for r, h in each:
        biased = [scores[r, h][cut] + ref[h] for cut, ref in zip(cuts, bias_refs)]
        biased = jnp.concatenate(biased, axis=0)
        weights = jnp.exp(biased - jnp.max(biased, axis=-1, keepdims=True))
        attention[r, h] = weights * (1.0 / jnp.sum(weights, axis=-1, keepdims=True))
        low[r, h] = attention[r, h].astype(BF16)
    attended = [jnp.zeros(lane.shape, F32) for _ in rows]
    for r, h in each:
        attended[r] = jnp.where(own(h, half), dot(low[r, h], kvs[r]), attended[r])
    edge = [ge * att for ge, att in zip(ges, attended)]
    d_low = {}
    for h in heads:
        total = None
        for r in range(len(rows)):
            delta = jnp.sum(jnp.where(own(h, half), edge[r], 0.0), axis=-1, keepdims=True)
            d_scores = attention[r, h] * (d_probs[r, h] - delta)
            total = d_scores if total is None else total + d_scores
            d_low[r, h] = d_scores.astype(BF16)
        for cut, ref in zip(cuts, dbias_refs):
            ref[h] += total[cut]
    results = []
    for r in range(len(rows)):
        gate = pltpu.roll(ges[r], half, 1)
        dqg = edge[r] * (1.0 - gate)
        for h in heads:
            dqg = jnp.where(own(h, 0), dot(d_low[r, h], kvs[r]) * scale_q, dqg)
        d_key = [dot(qd_t[r][h * head_dim : (h + 1) * head_dim], d_low[r, h]) for h in heads]
        d_value = [dot(qd_t[r][half + h * head_dim : half + (h + 1) * head_dim], low[r, h]) for h in heads]
        mixed = jnp.where(lane >= half, gate * attended[r], 0.0)
        results.append((dqg, mixed, jnp.concatenate(d_key + d_value, axis=0)))
    return results


def clear(refs):
    @pl.when(pl.program_id(0) == 0)
    def _():
        for ref in refs:
            ref[...] = jnp.zeros_like(ref)


def places(where_ref, order, n_z, rows_j):
    at = [lax.rem(where_ref[1] + s, n_z) * 2 + lax.rem(where_ref[2] + t, 2) for s, t in order]
    return [pl.ds(pl.multiple_of(p * rows_j, rows_j), rows_j) for p in at]


def first_kernel(half, head_dim, scale_q, order, n_z, n_now, where_ref, own_ref, other_ref, live_ref, w_in_ref, w_dm_ref, *refs):
    bias_refs, refs = refs[:n_now], refs[n_now:]
    (qd_ref, kv_ref, kvm_ref, ge_ref, dqg_ref, mix_ref, dkv_ref), refs = refs[:7], refs[7:]
    out_refs, (qd_s, ge_s), dbias_refs = refs[:n_now], refs[n_now : n_now + 2], refs[n_now + 2 :]
    clear(dbias_refs)
    weights = (w_in_ref[...], w_dm_ref[...])
    first = where_ref[0] == 0
    rows_j = bias_refs[0].shape[1] // 2
    now = slice(0, dqg_ref.shape[1])
    at = places(where_ref, order, n_z, rows_j)
    rows = []
    for r in range(qd_ref.shape[0]):
        qd, kv, kvm, ge = project(half, scale_q, first, own_ref[:, r], other_ref[:, r], live_ref[...], *weights)
        kv_ref[r] = kv
        kvm_ref[r] = kvm
        qd_s[r] = qd
        ge_s[r] = ge
        for n, p in enumerate(at):
            here = slice(n * rows_j, (n + 1) * rows_j)
            qd_ref[r, here] = qd_s[r, p]
            ge_ref[r, here] = ge_s[r, p]
        rows.append((qd_ref[r, now], ge_ref[r, now], kv, kvm))
    for r, (dqg, mixed, dkv) in enumerate(attend(half, head_dim, scale_q, rows, bias_refs, dbias_refs)):
        dqg_ref[r] = dqg
        dkv_ref[r] = dkv
        mix_ref[r] = mixed.astype(BF16)
    hand_over(dbias_refs, out_refs)


def middle_kernel(half, head_dim, scale_q, at, where_ref, qd_ref, kv_ref, kvm_ref, ge_ref, far_bias_ref, own_bias_ref, dkv_in_ref, *refs):
    dqg_ref, mix_ref, dkv_ref, near_ref, far_ref, own_ref, dbias_ref = refs
    clear([dbias_ref, own_ref])
    rows = [(qd_ref[r, at], ge_ref[r, at], kv_ref[r], kvm_ref[r]) for r in range(qd_ref.shape[0])]
    results = attend(half, head_dim, scale_q, rows, [far_bias_ref, own_bias_ref], [dbias_ref, own_ref])
    for r, (dqg, mixed, dkv) in enumerate(results):
        dqg_ref[r] = dqg
        dkv_ref[r] = dkv_in_ref[r] + dkv
        mix_ref[r] = mixed.astype(BF16)

    @pl.when(pl.program_id(0) == pl.num_programs(0) - 1)
    def _():
        rows_j = near_ref.shape[1]
        put_lines(dbias_ref[:, :rows_j], near_ref)
        put_lines(dbias_ref[:, rows_j:], far_ref)


def last_kernel(half, head_dim, scale_q, order, n_z, where_ref, qd_ref, kv_ref, kvm_ref, ge_ref, bias_ref, dqg_ref, mix_ref, dqg2_ref, mix2_ref, dkv_ref, w_back_ref, *refs):
    (keep_dn_ref, give_dn_ref, keep_mix_ref, give_mix_ref, dbias_ref, dn_s, mix_s) = refs
    clear([dbias_ref])
    rows = [(qd_ref[r], ge_ref[r], kv_ref[r], kvm_ref[r]) for r in range(qd_ref.shape[0])]
    results = attend(half, head_dim, scale_q, rows, [bias_ref], [dbias_ref])
    first = where_ref[0] == 0
    w_back = w_back_ref[...]
    rows_j = bias_ref.shape[1]
    at = places(where_ref, order, n_z, rows_j)
    chips, _, cells, width = keep_dn_ref.shape
    for r, (dqg, mixed, dkv) in enumerate(results):
        dn_s[r] = dot_exact((dkv + dkv_ref[r]).T, w_back[2 * half :])
        from_queries = dot_exact(jnp.concatenate([dqg_ref[r], dqg2_ref[r], dqg], axis=0), w_back[: 2 * half])
        mixed = jnp.concatenate([mix_ref[r].astype(F32), mix2_ref[r].astype(F32), mixed], axis=0)
        mixed = jnp.where(first, pltpu.roll(mixed, half, 1), mixed)
        for n, p in enumerate(at):
            here = slice(n * rows_j, (n + 1) * rows_j)
            dn_s[r, p] += from_queries[here]
            mix_s[r, p] = mixed[here]
        d_normed = dn_s[r].reshape(chips, 2, cells, width)
        mixed = mix_s[r].reshape(chips, 2, cells, width)
        keep_dn_ref[:, r] = jnp.where(first, d_normed[:, 0], d_normed[:, 1])
        give_dn_ref[:, r] = jnp.where(first, d_normed[:, 1], d_normed[:, 0])
        keep_mix_ref[:, r] = jnp.where(first, mixed[:, 0], mixed[:, 1]).astype(BF16)
        give_mix_ref[:, r] = jnp.where(first, mixed[:, 1], mixed[:, 0]).astype(BF16)


def merge_kernel(where_ref, keep_dn_ref, came_dn_ref, keep_mix_ref, came_mix_ref, keep_lines_ref, came_lines_ref, out_ref):
    chips, rows, cells, width = keep_dn_ref.shape
    d_normed = keep_dn_ref[...] + came_dn_ref[...]
    d_normed = d_normed - d_normed[..., width - 1 :]
    mixed = keep_mix_ref[...].astype(F32) + came_mix_ref[...].astype(F32)
    first = where_ref[0] == 0
    keep, came = (ref[...].astype(jnp.int32) for ref in (keep_lines_ref, came_lines_ref))
    lines = (jnp.where(first, keep, came), jnp.where(first, came, keep))
    lane = lanes((cells, width))
    for c in range(chips):
        scales = []
        for values in (d_normed, mixed):
            most = jnp.max(jnp.max(jnp.abs(values[c]), axis=0), axis=-1, keepdims=True)
            scales.append(jnp.broadcast_to(exponents(most), (cells, width)))
        slots = [s.astype(jnp.int32) for s in scales] + [line[c, :, width:] for line in lines]
        for r in range(rows):
            codes = encode(d_normed[c, r], scales[0])
            if r < len(slots):
                codes = jnp.where(lane == width - 1, slots[r], codes)
            out_ref[c, r, :, :width] = codes.astype(jnp.int16)
            out_ref[c, r, :, width:] = encode(mixed[c, r], scales[1]).astype(jnp.int16)
        for n in range(2):
            out_ref[c, rows, :, n * width : (n + 1) * width] = lines[n][c, :, :width].astype(jnp.int16)


def finish_kernel(pair_ref, came_ref, scales_ref, lines_ref, w_out_ref, w_spread_ref, update_ref, dpair_ref, dbias_s):
    rows, cells, width = pair_ref.shape
    chips, chip_rows = came_ref.shape[0], came_ref.shape[1] - 1
    flat = (rows * cells, width)
    lanes_of_head = w_spread_ref.shape[0] // 4
    step = pl.program_id(0)
    last = lanes((cells, width)) == width - 1

    def slot(line):
        line = line.astype(jnp.int32).astype(F32)
        return jnp.sum(jnp.where(last, line, 0.0), axis=-1, keepdims=True)

    @pl.when(step == 0)
    def _():
        for c in range(2):
            at = slice(c * width, (c + 1) * width)
            total = jnp.zeros((cells, width), F32)
            for n in range(lines_ref.shape[0]):
                total = total + decode(lines_ref[n, 0, :, at], slot(scales_ref[n, c, :, :width]))
            dbias_s[:, c * width : (c + 1) * width] = total

    normed, inverse = normalize(pair_ref[...].reshape(flat))
    came = []
    for n in range(2):
        parts = []
        for c in range(chips):
            scale = slot(came_ref[c, n, :, :width])
            for r in range(chip_rows):
                part = decode(came_ref[c, r, :, n * width : (n + 1) * width], scale)
                parts.append(jnp.where(last, 0.0, part) if n == 0 else part)
        came.append(jnp.concatenate(parts, axis=0))
    update_ref[...] = dot(came[1].astype(BF16), w_out_ref[...]).reshape(pair_ref.shape)
    d_bias = dbias_s[...]
    own = lax.rem(lanes(d_bias.shape), lanes_of_head)
    picked = [jnp.where(own == step * rows + r, d_bias, 0.0) for r in range(rows)]
    picked = jnp.concatenate(picked, axis=0)
    from_bias = jnp.zeros(flat, F32)
    for _ in range(3):
        high = picked.astype(BF16)
        from_bias = from_bias + dot(high, w_spread_ref[...])
        picked = picked - high.astype(F32)
    d_normed = came[0] + from_bias
    first_mean = jnp.mean(d_normed, axis=-1, keepdims=True)
    second_mean = jnp.mean(d_normed * normed, axis=-1, keepdims=True)
    dpair_ref[...] = (inverse * (d_normed - first_mean - normed * second_mean)).reshape(pair_ref.shape)


def shifted(array, axis, step):
    size = lax.axis_size(axis)
    return lax.ppermute(array, axis, [(s, (s + step) % size) for s in range(size)])


def kernel(fn, grid, in_specs, out_specs, out_shape, micros, name, scalars=0, scratch=(), aliases=None, vmem=24):
    return pl.pallas_call(
        fn,
        grid_spec=pltpu.PrefetchScalarGridSpec(
            num_scalar_prefetch=scalars, grid=grid, in_specs=in_specs, out_specs=out_specs, scratch_shapes=scratch
        ),
        out_shape=out_shape,
        input_output_aliases=aliases or {},
        compiler_params=pltpu.CompilerParams(vmem_limit_bytes=vmem * 1024 * 1024),
        cost_estimate=pl.CostEstimate(flops=int(micros * 1.1e9), bytes_accessed=int(micros * 2e6), transcendentals=0),
        name=name,
    )


def body(pair_act, token_mask, w_proj, w_bias, w_out, cotangent):
    rows, cells, width = pair_act.shape
    n_heads = w_bias.shape[1]
    head_dim = w_proj.shape[2] // n_heads
    my_heads = n_heads // 2
    half = my_heads * head_dim
    scale_q = 1.0 / math.sqrt(head_dim)
    nx, nyl, nz = (lax.axis_size(a) for a in ("x", "yl", "z"))
    chips = nx * nyl
    own_rows = rows // chips
    n_tokens = chips * 2 * cells
    core, z_at, yh_at = lax.axis_index("c"), lax.axis_index("z"), lax.axis_index("yh")
    cell_at = lax.axis_index(CELL)
    where = jnp.stack([core, z_at, yh_at])
    shape = jax.ShapeDtypeStruct

    def fixed(dims):
        return pl.BlockSpec(dims, lambda r, *w: (0,) * len(dims))

    def by_rows(count):
        return pl.BlockSpec((count * own_rows, cells, width), lambda r: (r, 0, 0))
    anywhere = pl.BlockSpec(memory_space=pl.ANY)

    live_here = lax.dynamic_slice_in_dim(token_mask, cell_at * cells, cells)
    live_here = jnp.broadcast_to(live_here[:, None], (cells, width))
    w_spread = jnp.repeat(w_bias, rows, axis=1)
    n_cells = chips * 2
    vmem = pl.BlockSpec(memory_space=pltpu.VMEM)
    cells_of = (2 * n_cells, cells, my_heads * rows)
    sent, bias = kernel(
        prepare_kernel, (chips // GP,),
        [by_rows(GP)] * 2 + [fixed(live_here.shape), fixed(w_spread.shape)],
        [pl.BlockSpec((GP, own_rows, cells, 2 * width), lambda r: (r, 0, 0, 0)), fixed(cells_of)],
        [shape((chips, own_rows, cells, 2 * width), BF16), shape(cells_of, F32)],
        3, "prepare",
    )(pair_act, cotangent, live_here, w_spread)

    bias = lax.all_to_all(bias, NEAR, 0, 0)
    sent = kernel(
        after_kernel, (), [anywhere, anywhere], anywhere, shape(sent.shape, sent.dtype), 0.1, "after", aliases={0: 0}
    )(sent, bias)
    block_shape = (my_heads, 2 * rows, n_tokens)
    block = kernel(
        turn_kernel, (1,), [fixed((2, n_tokens, my_heads * rows))], fixed(block_shape),
        shape(block_shape, F32), 1, "turn", scalars=1,
    )(where, bias.reshape(2, n_tokens, my_heads * rows))
    order = [(1, 0), (1, 1), (nz - 1, 0), (nz - 1, 1), (2, 0), (2, 1), (0, 1), (0, 0)]
    n_now = 2
    after_it = shifted(block, "z", 1)
    before_it = shifted(block, "z", nz - 1)
    bias_of = [before_it, after_it, shifted(block, "z", nz - 2)]

    w_in, w_back, w_dm = kernel(
        functools.partial(weights_kernel, half), (1,), [fixed(w_proj.shape), fixed(w_out.shape)],
        [fixed((width, 4 * half)), fixed((4 * half, width)), fixed((width, 2 * half))],
        [shape((width, 4 * half), BF16), shape((4 * half, width), BF16), shape((width, 2 * half), BF16)],
        1, "weights", scalars=1,
    )(where, w_proj, w_out)
    live = jnp.broadcast_to(token_mask[:, None], (n_tokens, 2 * half))

    own = lax.all_to_all(sent, CHIP, 0, 0)
    own = kernel(
        after_kernel, (), [anywhere] * 5, anywhere, shape(own.shape, own.dtype), 0.1, "after_own", aliases={0: 0}
    )(own, bias_of[1], bias_of[0], w_in, live)
    other = shifted(own, "c", 1)

    lane_shape = (own_rows, n_tokens, 2 * half)
    n_first = n_now * 2 * rows
    first_shape = (own_rows, n_first, 2 * half)
    cell_shape = (chips, own_rows, cells, width)
    blocks = [fixed(block_shape)] * n_now
    block_out = shape(block_shape, F32)
    coded_shape = block_shape[:2] + (n_tokens + 128,)
    coded_out = shape(coded_shape, jnp.int16)

    def of_rows(count, tokens, at=0):
        return pl.BlockSpec((count, tokens, 2 * half), lambda r, w: (r, at, 0))

    def of_cells(count, lanes_here):
        return pl.BlockSpec((chips, count, cells, lanes_here), lambda r, w: (0, r, 0, 0))

    def dkv_of(count):
        return pl.BlockSpec((count, 2 * half, n_tokens), lambda r, w: (r, 0, 0))

    qd, kv, kvm, ge, dqg, mix, dkv, *d_bias = kernel(
        functools.partial(first_kernel, half, head_dim, scale_q, order, nz, n_now), (own_rows // RA,),
        [of_cells(RA, 2 * width)] * 2 + [fixed(live.shape), fixed(w_in.shape), fixed(w_dm.shape)] + blocks,
        [of_rows(RA, n_tokens)] * 4 + [of_rows(RA, n_first)] * 2 + [dkv_of(RA)] + [fixed(coded_shape)] * n_now,
        [shape(lane_shape, t) for t in (BF16, BF16, BF16, F32)]
        + [shape(first_shape, t) for t in (F32, BF16)]
        + [shape((own_rows, 2 * half, n_tokens), F32)]
        + [coded_out] * n_now,
        20, "first", scalars=1, vmem=60, scratch=[pltpu.VMEM((RA, n_tokens, 2 * half), t) for t in (BF16, F32)] + [pltpu.VMEM(block_shape, F32)] * n_now,
    )(where, own, other, live, w_in, w_dm, *bias_of[:n_now])
    came = [shifted(d, "z", s) for d, s in zip(d_bias, (1, nz - 1))]
    n_middle = 3 * rows
    middle_rows = of_rows(RB, n_middle)
    middle_shape = (own_rows, n_middle, 2 * half)
    half_shape = (my_heads, rows, n_tokens)
    lines_out = (my_heads, rows, n_tokens + 128)
    near_half = pl.BlockSpec(half_shape, lambda r, w: (0, 0, 0))
    far_half = pl.BlockSpec(half_shape, lambda r, w: (0, 1, 0))
    whole_row = of_rows(RB, n_tokens)
    dqg2, mix2, dkv, d_near, d_far, d_own = kernel(
        functools.partial(middle_kernel, half, head_dim, scale_q, slice(n_first, n_first + n_middle)), (own_rows // RB,),
        [whole_row] * 4 + [fixed(block_shape), far_half, dkv_of(RB)],
        [middle_rows, middle_rows, dkv_of(RB), fixed(lines_out), fixed(lines_out), fixed(half_shape)],
        [shape(middle_shape, F32), shape(middle_shape, BF16), shape(dkv.shape, F32)]
        + [shape(lines_out, jnp.int16)] * 2 + [shape(half_shape, F32)],
        0.1, "middle", scalars=1, vmem=60, scratch=[pltpu.VMEM(block_shape, F32)],
    )(where, qd, kv, kvm, ge, bias_of[2], block, dkv)
    across = [(s, (s // 2 + 2) % nz * 2 + 1 - s % 2) for s in range(2 * nz)]
    came_near, came_far = shifted(d_near, "z", 2), lax.ppermute(d_far, ("z", "yh"), across)
    d_own = kernel(
        far_kernel, (1,), [fixed(half_shape)] + [fixed(coded_shape)] * 2, fixed(lines_out), shape(lines_out, jnp.int16),
        0.1, "far",
    )(d_own, *came)
    came_own = shifted(d_own, "yh", 1)
    last = of_rows(RL, rows, n_tokens // rows - 1)
    keep_dn, give_dn, keep_mix, give_mix, d_here = kernel(
        functools.partial(last_kernel, half, head_dim, scale_q, order, nz), (own_rows // RL,),
        [last, of_rows(RL, n_tokens), of_rows(RL, n_tokens), last, near_half]
        + [of_rows(RL, n_first)] * 2 + [of_rows(RL, n_middle)] * 2 + [dkv_of(RL), fixed(w_back.shape)],
        [of_cells(RL, width)] * 4 + [fixed(half_shape)],
        [shape(cell_shape, t) for t in (F32, F32, BF16, BF16)] + [shape(half_shape, F32)],
        0.1, "last", scalars=1, vmem=60,
        scratch=[pltpu.VMEM((RL, n_tokens, 2 * half), F32)] * 2,
    )(where, qd, kv, kvm, ge, block, dqg, mix, dqg2, mix2, dkv, w_back)

    lines_shape = (chips, cells, 2 * width)
    keep_lines, give_lines = kernel(
        lines_kernel, (1,), [fixed(half_shape)] + [fixed(lines_out)] * 5, [fixed(lines_shape)] * 2,
        [shape(lines_shape, jnp.int16)] * 2, 1, "lines", scalars=1,
    )(where, d_here, *came, came_near, came_far, came_own)
    came_lines = shifted(give_lines, "c", 1)

    give_dn, give_mix = kernel(
        after_kernel, (), [anywhere] * 5, [anywhere] * 2,
        [shape(cell_shape, F32), shape(cell_shape, BF16)], 0.1, "after_give", aliases={0: 0, 1: 1},
    )(give_dn, give_mix, came_near, came_far, came_own)
    came_dn, came_mix = shifted(give_dn, "c", 1), shifted(give_mix, "c", 1)
    cell_block = pl.BlockSpec((GM, own_rows, cells, width), lambda r, w: (r, 0, 0, 0))
    line_block = pl.BlockSpec((GM, cells, 2 * width), lambda r, w: (r, 0, 0))

    def wide_block(count):
        return pl.BlockSpec((count, own_rows + 1, cells, 2 * width), lambda r, *w: (r, 0, 0, 0))

    merged = kernel(
        merge_kernel, (chips // GM,), [cell_block] * 4 + [line_block] * 2, wide_block(GM),
        shape((chips, own_rows + 1, cells, 2 * width), jnp.int16), 2, "merge", scalars=1,
    )(where, keep_dn, came_dn, keep_mix, came_mix, keep_lines, came_lines)
    back = lax.all_to_all(merged, CHIP, 0, 0)

    def rows_of(count, at):
        return pl.BlockSpec((chips, count, cells, 2 * width), lambda r: (0, at, 0, 0))

    return kernel(
        finish_kernel, (chips // GF,),
        [by_rows(GF), wide_block(GF), rows_of(2, 1), rows_of(1, own_rows), fixed(w_out.shape), fixed((n_heads * rows, width))],
        [by_rows(GF)] * 2,
        [shape(pair_act.shape, F32)] * 2,
        3, "finish", scratch=[pltpu.VMEM((cells, n_heads * rows), F32)],
    )(pair_act, back, back, back, w_out, w_spread.T)


def solution(mesh):
    fine = Mesh(mesh.devices.reshape(4, 2, 4, 2, 2), ("z", "yh", "x", "yl", "c"))
    cells = P(("z", "yh"), CELL, None)
    return jax.shard_map(
        body,
        mesh=fine,
        in_specs=(cells, P(), P(), P(), P(), cells),
        out_specs=(cells, cells),
        check_vma=False,
    )
```
